256 devices in a mesh: ctx: 64 (over z, y, core), tp: 4 (over x).
Axes of the slice: x: 4, y: 4, z: 8, core: 2. Of those that a mesh axis runs over, the one named last changes fastest.
Arguments:
- xs: bfloat16 [8192, 8192], P(('ctx', 'tp')), may hold values from -6 to 6
- dts: bfloat16 [8192, 128], P(('ctx', 'tp')), may hold values from 0 to 0.35, as said below
- bs: bfloat16 [8192, 1024], P(('ctx', 'tp')), may hold values from -6 to 6
- cs: bfloat16 [8192, 1024], P(('ctx', 'tp')), may hold values from -6 to 6
- rates: float32 [128], P('tp'), may hold values from 0.5 to 2
- skips: float32 [128], P('tp'), may hold values from 0.5 to 1.5
- queries: bfloat16 [8192, 4096], P(('ctx', 'tp')), may hold values from -6 to 6
- keys: bfloat16 [8192, 1024], P(('ctx', 'tp')), may hold values from -6 to 6
- values: bfloat16 [8192, 1024], P(('ctx', 'tp')), may hold values from -6 to 6
- lengths: int32 [64], replicated, may hold values from 1 to 2048, 8192 in all
- grad_y: bfloat16 [8192, 8192], P(('ctx', 'tp')), may hold values from -6 to 6
- grad_attn: bfloat16 [8192, 4096], P(('ctx', 'tp')), may hold values from -6 to 6
Outputs:
- mixed_y: bfloat16 [8192, 8192], P(('ctx', 'tp'))
- grad_x: bfloat16 [8192, 8192], P(('ctx', 'tp'))
- grad_b: bfloat16 [8192, 1024], P(('ctx', 'tp'))
- grad_c: bfloat16 [8192, 1024], P(('ctx', 'tp'))
- attended: bfloat16 [8192, 4096], P(('ctx', 'tp'))
- grad_q: bfloat16 [8192, 4096], P(('ctx', 'tp'))
- grad_k: bfloat16 [8192, 1024], P(('ctx', 'tp'))
- grad_v: bfloat16 [8192, 1024], P(('ctx', 'tp'))
The draws below stay inside these ranges and needn't reach their ends.
Inputs may be any that keep to these rules, and one draw needn't show every extreme that they name: `lengths`: 64 documents in order that together cover all 8192 tokens; one of them is exactly 2048 tokens long. `dts`: positive step sizes.
All inputs are finite; a program needn't handle non-finite values.
Results may differ from the reference program's by a relative error of at most 0.034.
Values may be sent and summed in bfloat16 or wider, within the bound.
No kernel may reach another device: no remote copies, remote signals or barrier semaphores. Data moves between devices by JAX's collectives and lax.ppermute only.
A program may use at most 384 MiB of HBM per device.

```python
import math
import jax
import jax.numpy as jnp
import numpy as np
from jax import lax

MHEADS = 128
HEAD_P = 64
STATE = 128
GROUPS = 8
QHEADS = 32
KVHEADS = 8
HEAD_D = 128
TOKENS_PER_SHARD = 128
SPAN = 16
PACKED_TOKENS = 8192
MAXDOC = 2048
DOCS = 64
N_CTX = 64


def head_rates(key):
    low = jnp.log(0.5)
    high = jnp.log(2.0)
    return jnp.exp(jax.random.uniform(jax.random.fold_in(key, 201), (MHEADS,), minval=low, maxval=high))


def draw_queries(key, part):
    key = jax.random.fold_in(key, 5)
    final_output = jnp.clip(jax.random.normal(key, (PACKED_TOKENS, QHEADS * HEAD_D)), -6.0, 6.0)
    return final_output.astype(jnp.bfloat16)


def draw_keys(key, part):
    key = jax.random.fold_in(key, 6)
    final_output = jnp.clip(jax.random.normal(key, (PACKED_TOKENS, KVHEADS * HEAD_D)), -6.0, 6.0)
    return final_output.astype(jnp.bfloat16)


def draw_rates(key, part):
    shared_rates = head_rates(key)
    return shared_rates.astype(jnp.float32)


def draw_dts(key, part):
    shared_rates = head_rates(key)
    key = jax.random.fold_in(key, 7)
    random_key_split = jax.random.split(key, 6)
    fast_share = 0.5
    fast = jax.random.uniform(random_key_split[0], (MHEADS,)) < fast_share
    slow_total = jax.random.uniform(random_key_split[1], (MHEADS,), minval=0.4, maxval=1.2)
    slow_level = slow_total / ((SPAN + 1) * TOKENS_PER_SHARD)
    fast_level = 1.0 / jax.random.uniform(random_key_split[2], (MHEADS,), minval=40.0, maxval=56.0)
    signal_level = jnp.where(fast, fast_level, slow_level) / shared_rates
    coarse_estimate = jax.random.uniform(random_key_split[3], (PACKED_TOKENS, MHEADS), minval=0.5, maxval=1.5)
    block_multiplier = jnp.exp(jax.random.uniform(random_key_split[4], (PACKED_TOKENS // TOKENS_PER_SHARD, MHEADS), minval=jnp.log(0.6), maxval=jnp.log(1.4)))
    block_multiplier = jnp.repeat(block_multiplier, TOKENS_PER_SHARD, axis=0)
    sudden_spike = jax.random.uniform(random_key_split[5], (PACKED_TOKENS,)) < 1.0 / (8 * TOKENS_PER_SHARD)
    final_output = signal_level[None, :] * coarse_estimate * block_multiplier + jnp.where(sudden_spike[:, None], 0.3, 0.0)
    final_output = jnp.minimum(final_output, 0.35)
    return final_output.astype(jnp.bfloat16)


def block_levels(key, dims, pieces, low, top_value):
    factor_of, own = 1.0, jax.random.fold_in(key, 6)
    for axis_at, blocks in pieces:
        heights = jnp.exp(jax.random.uniform(jax.random.fold_in(own, axis_at), (blocks,), jnp.float32, low / len(pieces), top_value / len(pieces)))
        factor_of = factor_of * jnp.repeat(heights, dims[axis_at] // blocks).reshape([-1 if axis == axis_at else 1 for axis in range(len(dims))])
    return factor_of


def length_profile(count, total, most, lean):
    loads = [(1 << 20) // math.isqrt(grade ** lean) + 1 for grade in range(2, count + 1)]
    spare, given = total - most - (count - 1), [1] * (count - 1)
    while spare > 0:
        candidates = [i for i in range(count - 1) if given[i] < most]
        whole, budget = sum([loads[i] for i in candidates]), spare
        for i in candidates:
            extra = min(most - given[i], max(1, budget * loads[i] // whole), spare)
            given[i] = given[i] + extra
            spare = spare - extra
    return np.array([most] + given)


def ragged_sizes(rng, number_of, total, most, skew):
    if number_of == 2:
        one = jax.random.randint(rng, (), max(1, total - most), min(most, total - 1) + 1)
        return jnp.stack([one, total - one])
    tallies = jnp.asarray(length_profile(number_of, total, most, skew), jnp.int32)
    couples = (number_of - 1) // 2
    source_of, receiver = tallies[1:1 + 2 * couples:2], tallies[2:2 + 2 * couples:2]
    slack = jnp.minimum(source_of - 1, most - receiver)
    passed = jax.random.randint(jax.random.fold_in(rng, 1), (couples,), 0, 1 << 20) % (slack + 1)
    tallies = tallies.at[1:1 + 2 * couples:2].set(source_of - passed).at[2:2 + 2 * couples:2].set(receiver + passed)
    return tallies[jax.random.permutation(jax.random.fold_in(rng, 2), number_of)]


def noise(rng, extent, scale, most, pieces=(), kind=jnp.bfloat16):
    array = scale * jax.random.normal(rng, extent, jnp.float32)
    if pieces:
        array = array * block_levels(rng, extent, pieces, -0.22, 0.18)
    return jnp.clip(array, -most, most).astype(kind)


def setup_inputs(seed: int = 0) -> dict:
    seeds = jax.random.split(jax.random.key(seed), 13)
    return {
        "xs": noise(seeds[0], (PACKED_TOKENS, MHEADS * HEAD_P), 1.0, 6.0, ((0, 256),)),
        "dts": draw_dts(jax.random.fold_in(seeds[12], 71), 0),
        "bs": noise(seeds[2], (PACKED_TOKENS, GROUPS * STATE), 1.0, 6.0, ((0, 256),)),
        "cs": noise(seeds[3], (PACKED_TOKENS, GROUPS * STATE), 1.0, 6.0, ((0, 256),)),
        "rates": draw_rates(jax.random.fold_in(seeds[12], 71), 0),
        "skips": jnp.clip(0.5 + 1.0 * jax.random.uniform(seeds[5], (MHEADS,), jnp.float32) ** block_levels(seeds[5], (MHEADS,), ((0, 4),), -0.2, 0.2), 0.5, 1.5),
        "queries": draw_queries(jax.random.fold_in(seeds[12], 71), 0),
        "keys": draw_keys(jax.random.fold_in(seeds[12], 71), 0),
        "values": noise(seeds[8], (PACKED_TOKENS, KVHEADS * HEAD_D), 1.0, 6.0, ((0, 256),)),
        "lengths": ragged_sizes(seeds[9], DOCS, PACKED_TOKENS, MAXDOC, 2).astype(jnp.int32),
        "grad_y": noise(seeds[10], (PACKED_TOKENS, MHEADS * HEAD_P), 1.0, 6.0, ((0, 256),)),
        "grad_attn": noise(seeds[11], (PACKED_TOKENS, QHEADS * HEAD_D), 1.0, 6.0, ((0, 256),)),
    }


precise = lax.Precision.HIGHEST

def doc_ids(positions, lengths):
    ends = jnp.cumsum(lengths).astype(jnp.int32)
    return lax.optimization_barrier(jnp.sum((positions[:, None] >= ends[None, :]).astype(jnp.int32), axis=1)).astype(jnp.int32)

def block_decay(steps, rates):
    return jnp.cumsum(-(steps * rates[None, :]).T, axis=1)

def state_part(inputs, steps, b_proj, rates, documents, prior_doc, groups):
    cumul = block_decay(steps, rates)
    element_count, head_count = steps.shape
    model_width = inputs.shape[1] // head_count
    per_group = head_count // groups
    tail = documents == documents[element_count - 1]
    weight = jnp.where(tail[None, :], jnp.exp(cumul[:, element_count - 1:] - cumul), 0.0)
    scaled = (inputs.reshape(element_count, head_count, model_width) * (steps * weight.T)[:, :, None]).astype(jnp.bfloat16)
    state = jnp.einsum('lgrp,lgn->grpn', scaled.reshape(element_count, groups, per_group, model_width), b_proj.astype(jnp.bfloat16).reshape(element_count, groups, -1), preferred_element_type=jnp.float32)
    carry_rate = jnp.where(documents[element_count - 1] == prior_doc, jnp.exp(cumul[:, element_count - 1]), 0.0)
    return (state.reshape(head_count, model_width, -1), carry_rate)

def out_part(inputs, steps, b_proj, c_proj, incoming, rates, skips, documents, prior_doc, groups):
    cumul = block_decay(steps, rates)
    element_count, head_count = steps.shape
    model_width = inputs.shape[1] // head_count
    per_group = head_count // groups
    order = jnp.arange(element_count)
    same = (documents[:, None] == documents[None, :]) & (order[:, None] >= order[None, :])
    decay = jnp.exp(jnp.where(same[None], cumul[:, :, None] - cumul[:, None, :], -jnp.inf))
    b_groups = b_proj.astype(jnp.bfloat16).reshape(element_count, groups, -1)
    c_groups = c_proj.astype(jnp.bfloat16).reshape(element_count, groups, -1)
    scores = jnp.einsum('tgn,sgn->gts', c_groups, b_groups, preferred_element_type=jnp.float32)
    mixing_weight = (decay.reshape(groups, per_group, element_count, element_count) * scores[:, None]).astype(jnp.bfloat16)
    input_driven = (inputs.reshape(element_count, head_count, model_width) * steps[:, :, None]).astype(jnp.bfloat16)
    input_driven = input_driven.reshape(element_count, groups, per_group, model_width)
    inner_width = jnp.einsum('uyvq,quyn->vuyn', mixing_weight, input_driven, preferred_element_type=jnp.float32).reshape(element_count, head_count, model_width)
    state_low = incoming.astype(jnp.bfloat16).reshape(groups, per_group, model_width, -1)
    carried = jnp.einsum('tgn,grpn->tgrp', c_groups, state_low, preferred_element_type=jnp.float32).reshape(element_count, head_count, model_width)
    entry = jnp.where((documents == prior_doc)[:, None], jnp.exp(cumul.T), 0.0)
    final_output = inner_width + carried * entry[:, :, None] + skips[None, :, None] * inputs.reshape(element_count, head_count, model_width)
    return final_output.reshape(element_count, head_count * model_width)

def mamba_layer(inputs, steps, b_proj, c_proj, rates, skips, documents, prior_docs):

    def advance(state, block):
        x_block, t_block, b_block, c_block, d_block, p_block = block
        local, carry_rate = state_part(x_block, t_block, b_block, rates, d_block, p_block, GROUPS)
        output = out_part(x_block, t_block, b_block, c_block, state, rates, skips, d_block, p_block, GROUPS)
        return (carry_rate[:, None, None] * state + local, output)
    blocks = (inputs.reshape(N_CTX, TOKENS_PER_SHARD, -1), steps.reshape(N_CTX, TOKENS_PER_SHARD, -1), b_proj.reshape(N_CTX, TOKENS_PER_SHARD, -1), c_proj.reshape(N_CTX, TOKENS_PER_SHARD, -1), documents.reshape(N_CTX, TOKENS_PER_SHARD), prior_docs)
    start = jnp.zeros((MHEADS, HEAD_P, STATE), jnp.float32)
    _, outputs = lax.scan(jax.checkpoint(advance), start, blocks)
    return outputs.reshape(PACKED_TOKENS, -1)

def attention_layer(queries, keys, values, grad_attn, lengths):
    reach = SPAN * TOKENS_PER_SHARD
    window = reach + TOKENS_PER_SHARD
    per_kv = QHEADS // KVHEADS
    scale = HEAD_D ** (-0.5)
    front = jnp.zeros((reach, keys.shape[1]), keys.dtype)
    pad_keys = jnp.concatenate([front, keys], axis=0)
    pad_values = jnp.concatenate([front, values], axis=0)

    def by_query(block):
        start = (block * TOKENS_PER_SHARD).astype(jnp.int32)
        q_pos = start + jnp.arange(TOKENS_PER_SHARD, dtype=jnp.int32)
        k_pos = start - reach + jnp.arange(window, dtype=jnp.int32)
        mask = doc_ids(k_pos, lengths)[None, :] == doc_ids(q_pos, lengths)[:, None]
        mask = mask & (k_pos[None, :] <= q_pos[:, None]) & (k_pos[None, :] >= 0)
        q_rows = lax.dynamic_slice_in_dim(queries, start, TOKENS_PER_SHARD, 0).astype(jnp.float32)
        q_rows = q_rows.reshape(TOKENS_PER_SHARD, KVHEADS, per_kv, HEAD_D)
        g_rows = lax.dynamic_slice_in_dim(grad_attn, start, TOKENS_PER_SHARD, 0).astype(jnp.float32)
        g_rows = g_rows.reshape(TOKENS_PER_SHARD, KVHEADS, per_kv, HEAD_D)
        k_rows = lax.dynamic_slice_in_dim(pad_keys, start, window, 0).astype(jnp.float32).reshape(window, KVHEADS, HEAD_D)
        v_rows = lax.dynamic_slice_in_dim(pad_values, start, window, 0).astype(jnp.float32).reshape(window, KVHEADS, HEAD_D)
        scores = jnp.einsum('tkrd,skd->krts', q_rows, k_rows, precision=precise) * scale
        scores = jnp.where(mask[None, None], scores, -jnp.inf)
        peak = lax.optimization_barrier(jnp.max(scores, axis=-1))
        log_total = peak + jnp.log(lax.optimization_barrier(jnp.sum(jnp.exp(scores - peak[..., None]), axis=-1)))
        probs = jnp.exp(scores - log_total[..., None])
        rounded = lax.optimization_barrier(probs.astype(jnp.bfloat16)).astype(jnp.float32)
        output = jnp.einsum('krts,skd->tkrd', rounded, v_rows, precision=precise)
        output = output.reshape(TOKENS_PER_SHARD, -1).astype(jnp.bfloat16)
        delta = lax.optimization_barrier(jnp.sum(g_rows * output.astype(jnp.float32).reshape(TOKENS_PER_SHARD, KVHEADS, per_kv, HEAD_D), axis=-1))
        delta = delta.transpose(1, 2, 0)
        prob_grad = jnp.einsum('tkrd,skd->krts', g_rows, v_rows, precision=precise)
        score_grad = probs * (prob_grad - delta[..., None])
        score_grad = lax.optimization_barrier(score_grad.astype(jnp.bfloat16)).astype(jnp.float32)
        q_grad = jnp.einsum('krts,skd->tkrd', score_grad, k_rows, precision=precise) * scale
        return (output, log_total, delta, q_grad.reshape(TOKENS_PER_SHARD, -1).astype(jnp.bfloat16))
    blocks = jnp.arange(N_CTX, dtype=jnp.int32)
    attended, log_totals, deltas, q_grads = lax.map(by_query, blocks)
    log_all = jnp.concatenate([log_totals.transpose(1, 2, 0, 3).reshape(KVHEADS, per_kv, PACKED_TOKENS), jnp.zeros((KVHEADS, per_kv, reach), jnp.float32)], axis=2)
    delta_all = jnp.concatenate([deltas.transpose(1, 2, 0, 3).reshape(KVHEADS, per_kv, PACKED_TOKENS), jnp.zeros((KVHEADS, per_kv, reach), jnp.float32)], axis=2)
    back = jnp.zeros((reach, queries.shape[1]), queries.dtype)
    pad_queries = jnp.concatenate([queries, back], axis=0)
    pad_grads = jnp.concatenate([grad_attn, back], axis=0)

    def by_key(block):
        start = (block * TOKENS_PER_SHARD).astype(jnp.int32)
        k_pos = start + jnp.arange(TOKENS_PER_SHARD, dtype=jnp.int32)
        q_pos = start + jnp.arange(window, dtype=jnp.int32)
        mask = doc_ids(k_pos, lengths)[None, :] == doc_ids(q_pos, lengths)[:, None]
        mask = mask & (k_pos[None, :] <= q_pos[:, None]) & (q_pos[:, None] < PACKED_TOKENS)
        q_rows = lax.dynamic_slice_in_dim(pad_queries, start, window, 0).astype(jnp.float32)
        q_rows = q_rows.reshape(window, KVHEADS, per_kv, HEAD_D)
        g_rows = lax.dynamic_slice_in_dim(pad_grads, start, window, 0).astype(jnp.float32)
        g_rows = g_rows.reshape(window, KVHEADS, per_kv, HEAD_D)
        k_rows = lax.dynamic_slice_in_dim(keys, start, TOKENS_PER_SHARD, 0).astype(jnp.float32).reshape(TOKENS_PER_SHARD, KVHEADS, HEAD_D)
        v_rows = lax.dynamic_slice_in_dim(values, start, TOKENS_PER_SHARD, 0).astype(jnp.float32).reshape(TOKENS_PER_SHARD, KVHEADS, HEAD_D)
        log_rows = lax.dynamic_slice_in_dim(log_all, start, window, 2)
        delta_rows = lax.dynamic_slice_in_dim(delta_all, start, window, 2)
        scores = jnp.einsum('tkrd,skd->krts', q_rows, k_rows, precision=precise) * scale
        scores = jnp.where(mask[None, None], scores, -jnp.inf)
        probs = jnp.exp(scores - log_rows[..., None])
        rounded = lax.optimization_barrier(probs.astype(jnp.bfloat16)).astype(jnp.float32)
        prob_grad = jnp.einsum('tkrd,skd->krts', g_rows, v_rows, precision=precise)
        score_grad = probs * (prob_grad - delta_rows[..., None])
        score_grad = lax.optimization_barrier(score_grad.astype(jnp.bfloat16)).astype(jnp.float32)
        k_grad = jnp.einsum('krts,tkrd->skd', score_grad, q_rows, precision=precise) * scale
        v_grad = jnp.einsum('krts,tkrd->skd', rounded, g_rows, precision=precise)
        return (k_grad.reshape(TOKENS_PER_SHARD, -1).astype(jnp.bfloat16), v_grad.reshape(TOKENS_PER_SHARD, -1).astype(jnp.bfloat16))
    k_grads, v_grads = lax.map(by_key, blocks)
    return (attended.reshape(PACKED_TOKENS, -1), q_grads.reshape(PACKED_TOKENS, -1), k_grads.reshape(PACKED_TOKENS, -1), v_grads.reshape(PACKED_TOKENS, -1))

def reference(xs, dts, bs, cs, rates, skips, queries, keys, values, lengths, grad_y, grad_attn):
    positions = jnp.arange(PACKED_TOKENS, dtype=jnp.int32)
    documents = doc_ids(positions, lengths)
    block_start = jnp.arange(N_CTX, dtype=jnp.int32) * TOKENS_PER_SHARD
    prior_docs = jnp.where(block_start > 0, doc_ids(block_start - 1, lengths), -1).astype(jnp.int32)
    steps = dts.astype(jnp.float32)

    def forward(inputs, b_proj, c_proj):
        return mamba_layer(inputs, steps, b_proj, c_proj, rates, skips, documents, prior_docs)
    mixed, pull = jax.vjp(forward, xs.astype(jnp.float32), bs.astype(jnp.float32), cs.astype(jnp.float32))
    x_grad, b_grad, c_grad = pull(grad_y.astype(jnp.float32))
    attended, q_grad, k_grad, v_grad = attention_layer(queries, keys, values, grad_attn, lengths)
    return (mixed.astype(jnp.bfloat16), x_grad.astype(jnp.bfloat16), b_grad.astype(jnp.bfloat16), c_grad.astype(jnp.bfloat16), attended, q_grad, k_grad, v_grad)
```

```python
import jax
import jax.numpy as jnp
from jax import lax
from jax.experimental import pallas as pl
from jax.experimental.pallas import tpu as pltpu
from jax.sharding import Mesh, PartitionSpec as P

BF = jnp.bfloat16
F32 = jnp.float32
GROUP = ("y", "core", "tp")
ROWS = 32
SUPER = 1024
BLOCK = 128
BLOCKS = SUPER // BLOCK
HEADS = 4
WIDTH = 64
CH = HEADS * WIDTH
STATE = 128
LANES = 128
SCALE = 128 ** (-0.5)
TQ = 256
TK = 512
NEG = -1e30
VMEM = 60 * 1024 * 1024
NN = (((1,), (0,)), ((), ()))
NT = (((1,), (1,)), ((), ()))
TN = (((0,), (0,)), ((), ()))


def dot(a, b, dims=NN):
    return lax.dot_general(a, b, dims, preferred_element_type=F32)


def params():
    return pltpu.CompilerParams(vmem_limit_bytes=VMEM)


def smem():
    return pl.BlockSpec(memory_space=pltpu.SMEM)


def vmem():
    return pl.BlockSpec(memory_space=pltpu.VMEM)


def pack_mixer(x_ref, gy_ref, b_ref, c_ref, dt_ref, out_ref):
    for t in range(4):
        out_ref[t, :, 0:256] = x_ref[:, t * 256 : t * 256 + 256]
        out_ref[t, :, 256:512] = gy_ref[:, t * 256 : t * 256 + 256]
        out_ref[t, :, 512:640] = b_ref[...]
        out_ref[t, :, 640:768] = c_ref[...]
        out_ref[t, :, 768:896] = dt_ref[...]


def pack_attention(q_ref, ga_ref, k2, v2, k1, v1, k0, v0, out_ref):
    for t in range(4):
        out_ref[t, :, 0:128] = q_ref[:, t * 128 : t * 128 + 128]
        out_ref[t, :, 128:256] = ga_ref[:, t * 128 : t * 128 + 128]
        for n, ref in enumerate((k2, v2, k1, v1, k0, v0)):
            out_ref[t, :, 256 + n * 128 : 384 + n * 128] = ref[...]


def wide(width, place=0):
    return pl.BlockSpec((ROWS, width), lambda g: (0, g + place))


def do_pack_mixer(xs, gy, bs, cs, dts):
    return pl.pallas_call(
        pack_mixer,
        grid=(8,),
        in_specs=[wide(1024), wide(1024), wide(128), wide(128), pl.BlockSpec((ROWS, 128), lambda g: (0, 0))],
        out_specs=pl.BlockSpec((4, ROWS, 896), lambda g: (g, 0, 0)),
        out_shape=jax.ShapeDtypeStruct((32, ROWS, 896), BF),
        compiler_params=params(),
    )(xs, gy, bs, cs, dts)


def do_pack_attention(q, ga, kv2, kv1, kv0):
    return pl.pallas_call(
        pack_attention,
        grid=(8,),
        in_specs=[wide(512), wide(512)] + [wide(128), wide(128, 8)] * 3,
        out_specs=pl.BlockSpec((4, ROWS, 1024), lambda g: (g, 0, 0)),
        out_shape=jax.ShapeDtypeStruct((32, ROWS, 1024), BF),
        compiler_params=params(),
    )(q, ga, kv2, kv2, kv1, kv1, kv0, kv0)


def unpack_mixer(in_ref, y_ref, gx_ref, gb_ref, gc_ref):
    gb = jnp.zeros((ROWS, 128), F32)
    gc = jnp.zeros((ROWS, 128), F32)
    for t in range(4):
        y_ref[:, t * 256 : t * 256 + 256] = in_ref[t, :, 0:256]
        gx_ref[:, t * 256 : t * 256 + 256] = in_ref[t, :, 256:512]
        gb = gb + in_ref[t, :, 512:640].astype(F32)
        gc = gc + in_ref[t, :, 640:768].astype(F32)
    gb_ref[...] = gb.astype(BF)
    gc_ref[...] = gc.astype(BF)


def do_unpack_mixer(got):
    return pl.pallas_call(
        unpack_mixer,
        grid=(8,),
        in_specs=[pl.BlockSpec((4, ROWS, 768), lambda g: (g, 0, 0))],
        out_specs=[wide(1024), wide(1024), wide(128), wide(128)],
        out_shape=[
            jax.ShapeDtypeStruct((ROWS, 8192), BF),
            jax.ShapeDtypeStruct((ROWS, 8192), BF),
            jax.ShapeDtypeStruct((ROWS, 1024), BF),
            jax.ShapeDtypeStruct((ROWS, 1024), BF),
        ],
        compiler_params=params(),
    )(got)


def unpack_attention(in_ref, att_ref, gq_ref, kv2_ref, kv1_ref, kv0_ref):
    for t in range(4):
        att_ref[:, t * 128 : t * 128 + 128] = in_ref[t, :, 0:128]
        gq_ref[:, t * 128 : t * 128 + 128] = in_ref[t, :, 128:256]
    for n, ref in enumerate((kv2_ref, kv1_ref, kv0_ref)):
        total = in_ref[0, :, 256 + n * 256 : 512 + n * 256].astype(F32)
        for t in range(1, 4):
            total = total + in_ref[t, :, 256 + n * 256 : 512 + n * 256].astype(F32)
        ref[...] = total.astype(ref.dtype)


def do_unpack_attention(got):
    return pl.pallas_call(
        unpack_attention,
        grid=(8,),
        in_specs=[pl.BlockSpec((4, ROWS, 1024), lambda g: (g, 0, 0))],
        out_specs=[wide(512), wide(512), wide(256), wide(256), wide(256)],
        out_shape=[
            jax.ShapeDtypeStruct((ROWS, 4096), BF),
            jax.ShapeDtypeStruct((ROWS, 4096), BF),
            jax.ShapeDtypeStruct((ROWS, 2048), BF),
            jax.ShapeDtypeStruct((ROWS, 2048), BF),
            jax.ShapeDtypeStruct((ROWS, 2048), F32),
        ],
        compiler_params=params(),
    )(got)


def add_kv(own_ref, one_ref, two_ref, gk_ref, gv_ref):
    for g in range(8):
        at = slice(g * 256, g * 256 + 256)
        total = (own_ref[:, at] + one_ref[:, at].astype(F32) + two_ref[:, at].astype(F32)).astype(BF)
        gk_ref[:, g * 128 : g * 128 + 128] = total[:, 0:128]
        gv_ref[:, g * 128 : g * 128 + 128] = total[:, 128:256]


def do_add_kv(own, one, two):
    return pl.pallas_call(
        add_kv,
        in_specs=[vmem()] * 3,
        out_specs=[vmem()] * 2,
        out_shape=[jax.ShapeDtypeStruct((ROWS, 1024), BF)] * 2,
        compiler_params=params(),
    )(own, one, two)


def lane_row(values, width):
    lane = lax.broadcasted_iota(jnp.int32, (1, width * HEADS), 1)
    row = jnp.full((1, width * HEADS), values[0], F32)
    for h in range(1, HEADS):
        row = jnp.where(lane >= h * width, values[h], row)
    return row


def lower(n):
    return (
        lax.broadcasted_iota(jnp.int32, (n, n), 1) <= lax.broadcasted_iota(jnp.int32, (n, n), 0)
    ).astype(F32).astype(BF)


def upper(n):
    return (
        lax.broadcasted_iota(jnp.int32, (n, n), 0) <= lax.broadcasted_iota(jnp.int32, (n, n), 1)
    ).astype(F32).astype(BF)


def pick(first, width):
    head = lax.broadcasted_iota(jnp.int32, (128, width * HEADS), 0) - first
    lane = lax.broadcasted_iota(jnp.int32, (128, width * HEADS), 1) // width
    return (head == lane).astype(F32).astype(BF)


def channel_decay(dts, chooser, tri, rate_row, tail, entry):
    steps = dot(dts, chooser)
    cumul = dot(tri, steps.astype(BF)) * (-rate_row)
    end = cumul[BLOCK - 1 : BLOCK, :]
    row = lax.broadcasted_iota(jnp.int32, (BLOCK, CH), 0)
    weight = jnp.where(row >= tail, jnp.exp(end - cumul), 0.0)
    enter = jnp.where(row < entry, jnp.exp(cumul), 0.0)
    return steps, steps * weight, enter, end


def state_kernel(info, rates, in_ref, inc_ref, out_ref, factor_ref, sf_ref, sb_ref):
    first = info[3, 0] * HEADS
    tri = lower(BLOCK)
    chooser = pick(first, WIDTH)
    rate_row = lane_row([rates[h] for h in range(HEADS)], WIDTH)
    state = jnp.zeros((STATE, CH), F32)
    prefix = jnp.ones((1, CH), F32)
    carries = []
    pulled = []
    for j in range(BLOCKS):
        rows = slice(j * BLOCK, j * BLOCK + BLOCK)
        tail, entry, alive = info[0, j], info[1, j], info[2, j]
        _, weighted, enter, end = channel_decay(
            in_ref[rows, 768:896], chooser, tri, rate_row, tail, entry
        )
        scaled = (in_ref[rows, 0:256].astype(F32) * weighted).astype(BF)
        dcar = (in_ref[rows, 256:512].astype(F32) * enter).astype(BF)
        carry = jnp.where(alive > 0, jnp.exp(end), 0.0)
        inc_ref[j] = state
        factor_ref[j : j + 1, :] = prefix
        state = carry * state + dot(in_ref[rows, 512:640], scaled, TN)
        prefix = prefix * carry
        carries.append(carry)
        pulled.append(dot(in_ref[rows, 640:768], dcar, TN))
    high = prefix.astype(BF)
    low = (prefix - high.astype(F32)).astype(BF)
    place = lax.broadcasted_iota(jnp.int32, (16, CH), 0)
    extra = jnp.where(place == 0, high.astype(F32), jnp.where(place == 1, low.astype(F32), 0.0)).astype(BF)
    sf_ref[0:128, :] = state.astype(BF)
    sf_ref[128:144, :] = extra
    back = jnp.zeros((STATE, CH), F32)
    suffix = jnp.ones((1, CH), F32)
    for j in range(BLOCKS - 1, -1, -1):
        out_ref[j] = back
        factor_ref[8 + j : 9 + j, :] = suffix
        back = pulled[j] + carries[j] * back
        suffix = suffix * carries[j]
    sb_ref[0:128, :] = back.astype(BF)
    sb_ref[128:144, :] = extra


def do_state(info, rates, got):
    return pl.pallas_call(
        state_kernel,
        in_specs=[smem(), smem(), vmem()],
        out_specs=[vmem()] * 5,
        out_shape=[
            jax.ShapeDtypeStruct((BLOCKS, STATE, CH), F32),
            jax.ShapeDtypeStruct((BLOCKS, STATE, CH), F32),
            jax.ShapeDtypeStruct((16, CH), F32),
            jax.ShapeDtypeStruct((144, CH), BF),
            jax.ShapeDtypeStruct((144, CH), BF),
        ],
        compiler_params=params(),
    )(info, rates, got)


def joined(one_ref, two_ref):
    decay = one_ref[128:129, :].astype(F32) + one_ref[129:130, :].astype(F32)
    return one_ref[0:128, :].astype(F32) + decay * two_ref[0:128, :].astype(F32)


def mixer_kernel(
    info, rates, skips, in_ref, ends_ref, inc_ref, back_ref, factor_ref, f1, f2, b1, b2, out_ref
):
    first = info[3, 0] * HEADS
    tri = lower(BLOCK)
    triu = upper(BLOCK)
    chooser = pick(first, WIDTH)
    column_chooser = pick(first, LANES)
    head_row = lax.broadcasted_iota(jnp.int32, (8, 128), 0)
    head_at = lax.broadcasted_iota(jnp.int32, (8, 128), 1) - first
    row_chooser = ((head_row == head_at) & (head_row < HEADS)).astype(F32).astype(BF)
    rate_row = lane_row([rates[h] for h in range(HEADS)], WIDTH)
    skip_row = lane_row([skips[h] for h in range(HEADS)], WIDTH)
    entering = joined(f1, f2)
    leaving = joined(b1, b2)
    t_at = lax.broadcasted_iota(jnp.int32, (BLOCK, BLOCK), 0)
    s_at = lax.broadcasted_iota(jnp.int32, (BLOCK, BLOCK), 1)
    lane = lax.broadcasted_iota(jnp.int32, (BLOCK, CH), 1)
    owns = [(lane >= h * WIDTH) & (lane < (h + 1) * WIDTH) for h in range(HEADS)]

    def one(j, _):
        rows = pl.ds(pl.multiple_of(j * BLOCK, BLOCK), BLOCK)
        tail, entry = info[0, j], info[1, j]
        dts = in_ref[rows, 768:896]
        steps, weighted, enter, _ = channel_decay(dts, chooser, tri, rate_row, tail, entry)
        x = in_ref[rows, 0:256].astype(F32)
        gy_low = in_ref[rows, 256:512]
        gy = gy_low.astype(F32)
        b = in_ref[rows, 512:640]
        c = in_ref[rows, 640:768]
        state = (inc_ref[j] + factor_ref[pl.ds(j, 1), :] * entering).astype(BF)
        pull = (back_ref[j] + factor_ref[pl.ds(8 + j, 1), :] * leaving).astype(BF)
        columns = dot(tri, dot(dts, column_chooser).astype(BF))
        lines = dot(dot(row_chooser, dts, NT).astype(BF), triu)
        ends = ends_ref[pl.ds(j, 1), :]
        mask = (s_at <= t_at) & (t_at < ends)
        scores = dot(c, b, NT)
        driven = x * steps
        decays = []
        mixes = []
        drives = []
        for h in range(HEADS):
            gap = (columns[:, h * 128 : h * 128 + 128] - lines[h : h + 1, :]) * (-rates[h])
            decay = jnp.exp(jnp.where(mask, gap, NEG))
            decays.append(decay)
            mixes.append((decay * scores).astype(BF))
            drives.append(jnp.where(owns[h], driven, 0.0).astype(BF))
        mix = jnp.concatenate(mixes, axis=1)
        drive = jnp.concatenate(drives, axis=0)
        y = dot(mix, drive) + dot(c, state) * enter + skip_row * x
        out_ref[rows, 0:256] = y.astype(BF)
        grad_mix = dot(gy_low, drive, NT)
        grad_scores = decays[0] * grad_mix[:, 0:128]
        for h in range(1, HEADS):
            grad_scores = grad_scores + decays[h] * grad_mix[:, h * 128 : h * 128 + 128]
        grad_low = grad_scores.astype(BF)
        back = dot(mix, gy_low, TN)
        grad_drive = jnp.where(owns[0], back[0:128], 0.0)
        for h in range(1, HEADS):
            grad_drive = jnp.where(owns[h], back[h * 128 : h * 128 + 128], grad_drive)
        grad_scaled = dot(b, pull)
        gx = grad_drive * steps + grad_scaled * weighted + skip_row * gy
        out_ref[rows, 256:512] = gx.astype(BF)
        scaled = (x * weighted).astype(BF)
        dcar = (gy * enter).astype(BF)
        gb = dot(grad_low, c, TN) + dot(scaled, pull, NT)
        gc = dot(grad_low, b) + dot(dcar, state, NT)
        out_ref[rows, 512:640] = gb.astype(BF)
        out_ref[rows, 640:768] = gc.astype(BF)
        return 0

    lax.fori_loop(0, BLOCKS, one, 0)


def do_mixer(info, rates, skips, got, ends, inc, back, factor, f1, f2, b1, b2):
    return pl.pallas_call(
        mixer_kernel,
        in_specs=[smem()] * 3 + [vmem()] * 9,
        out_specs=vmem(),
        out_shape=jax.ShapeDtypeStruct((SUPER, 768), BF),
        compiler_params=params(),
    )(info, rates, skips, got, ends, inc, back, factor, f1, f2, b1, b2)


def attention_kernel(starts, in_ref, start_ref, out_ref, kt_ref, vt_ref, s_ref, acc_ref):
    tiles = 3 * SUPER // TK
    lowest = starts[0] // TK

    def key_at(t):
        rows = pl.ds(pl.multiple_of((t % 2) * TK, TK), TK)
        return rows, pl.multiple_of(256 + (t // 2) * 256, 256)

    def turn(t, _):
        rows, col = key_at(t)
        kt_ref[t] = in_ref[rows, pl.ds(col, 128)].T
        vt_ref[t] = in_ref[rows, pl.ds(col + 128, 128)].T
        return 0

    lax.fori_loop(lowest, tiles, turn, 0)
    acc_ref[...] = jnp.zeros_like(acc_ref)

    def one(i, _):
        rows = pl.ds(pl.multiple_of(i * TQ, TQ), TQ)
        q = in_ref[rows, 0:128]
        ga = in_ref[rows, 128:256]
        begin = start_ref[pl.ds(i, 1), :]
        here = 2 * SUPER + i * TQ + lax.broadcasted_iota(jnp.int32, (1, TQ), 1)
        low = starts[i * TQ] // TK
        high = (2 * SUPER + i * TQ + TQ - 1) // TK + 1

        def score(t, peak):
            krows, col = key_at(t)
            s = dot(in_ref[krows, pl.ds(col, 128)], q, NT) * SCALE
            at = t * TK + lax.broadcasted_iota(jnp.int32, (TK, TQ), 0)
            s = jnp.where((at >= begin) & (at <= here), s, NEG)
            s_ref[t] = s
            return jnp.maximum(peak, jnp.max(s.reshape(TK // 8, 8, TQ), axis=0))

        peak = lax.fori_loop(low, high, score, jnp.full((8, TQ), NEG, F32))
        peak = jnp.max(peak, axis=0, keepdims=True)

        def weigh(t, carry):
            total, att = carry
            p = jnp.exp(s_ref[t] - peak)
            s_ref[t] = p
            total = total + jnp.sum(p.reshape(TK // 8, 8, TQ), axis=0)
            return total, att + dot(vt_ref[t], p.astype(BF))

        total, att = lax.fori_loop(
            low, high, weigh, (jnp.zeros((8, TQ), F32), jnp.zeros((128, TQ), F32))
        )
        inverse = 1.0 / jnp.sum(total, axis=0, keepdims=True)
        att = (att * inverse).T.astype(BF)
        out_ref[rows, 0:128] = att
        delta = jnp.sum((ga.astype(F32) * att.astype(F32)).T, axis=0, keepdims=True)

        def grads(t, gq):
            krows, col = key_at(t)
            probs = s_ref[t] * inverse
            dp = dot(in_ref[krows, pl.ds(col + 128, 128)], ga, NT)
            ds = (probs * (dp - delta)).astype(BF)
            acc_ref[t, :, 0:128] += dot(ds, q)
            acc_ref[t, :, 128:256] += dot(probs.astype(BF), ga)
            return gq + dot(kt_ref[t], ds)

        gq = lax.fori_loop(low, high, grads, jnp.zeros((128, TQ), F32))
        out_ref[rows, 128:256] = (gq * SCALE).T.astype(BF)
        return 0

    lax.fori_loop(0, SUPER // TQ, one, 0)
    for t in range(tiles):
        rows = slice((t % 2) * TK, (t % 2) * TK + TK)
        col = 256 + (t // 2) * 256
        out_ref[rows, col : col + 128] = (acc_ref[t, :, 0:128] * SCALE).astype(BF)
        out_ref[rows, col + 128 : col + 256] = acc_ref[t, :, 128:256].astype(BF)


def do_attention(starts, got):
    tiles = 3 * SUPER // TK
    return pl.pallas_call(
        attention_kernel,
        in_specs=[smem(), vmem(), vmem()],
        out_specs=vmem(),
        out_shape=jax.ShapeDtypeStruct((SUPER, 1024), BF),
        scratch_shapes=[
            pltpu.VMEM((tiles, 128, TK), BF),
            pltpu.VMEM((tiles, 128, TK), BF),
            pltpu.VMEM((tiles, TK, TQ), F32),
            pltpu.VMEM((tiles, TK, 256), F32),
        ],
        compiler_params=params(),
    )(starts, got, starts.reshape(SUPER // TQ, TQ))


def shifted(block, distance):
    count = lax.axis_size("z")
    route = [(i, i + distance) for i in range(count) if 0 <= i + distance < count]
    return lax.ppermute(block, "z", route)


def exchange(block):
    return lax.all_to_all(block, GROUP, split_axis=0, concat_axis=0, tiled=True)


def per_device(xs, dts, bs, cs, rates, skips, queries, keys, values, lengths, grad_y, grad_attn):
    z, y, core, tp = (lax.axis_index(a) for a in ("z", "y", "core", "tp"))
    device = (y * 2 + core) * 4 + tp

    kv0 = jnp.concatenate([keys, values], axis=1)
    kv1 = shifted(kv0, 1)
    kv2 = shifted(kv0, 2)
    side = lax.axis_size("tp")
    both = lax.ppermute(
        jnp.stack([rates, skips]),
        ("y", "tp"),
        [(a * side + b, b * side + a) for a in range(side) for b in range(side)],
    )
    mine = lax.dynamic_slice_in_dim(both, core * 16 + tp * HEADS, HEADS, 1)
    my_rates, my_skips = mine[0], mine[1]

    ends = jnp.cumsum(lengths)
    begins = ends - lengths
    base = z * SUPER
    positions = base + jnp.arange(SUPER, dtype=jnp.int32)
    starts = jnp.max(jnp.where(begins[None, :] <= positions[:, None], begins[None, :], 0), axis=1)
    stops = jnp.min(
        jnp.where(ends[None, :] > positions[:, None], ends[None, :], SUPER * 8), axis=1
    )
    block_at = base + jnp.arange(BLOCKS, dtype=jnp.int32) * BLOCK
    last_start = starts[BLOCK - 1 :: BLOCK]
    prior_stop = jnp.min(
        jnp.where(ends[None, :] >= block_at[:, None], ends[None, :], SUPER * 8), axis=1
    )
    entry = jnp.where(block_at > 0, prior_stop - block_at, 0)
    info = jnp.stack(
        [
            last_start - block_at,
            entry,
            (last_start < block_at).astype(jnp.int32),
            jnp.full((BLOCKS,), device, jnp.int32),
        ]
    )
    local_stops = (stops.reshape(BLOCKS, BLOCK) - block_at[:, None]).astype(jnp.int32)

    got = exchange(do_pack_mixer(xs, grad_y, bs, cs, dts)).reshape(SUPER, 896)
    inc, back, factor, send_f, send_b = do_state(info, my_rates, got)
    f1, f2 = shifted(send_f, 1), shifted(send_f, 2)
    b1, b2 = shifted(send_b, -1), shifted(send_b, -2)

    got_a = exchange(do_pack_attention(queries, grad_attn, kv2, kv1, kv0)).reshape(SUPER, 1024)
    attended = do_attention((starts - (base - 2 * SUPER)).astype(jnp.int32), got_a)
    out_a = exchange(attended.reshape(32, ROWS, 1024))
    att, gq, p2, p1, p0 = do_unpack_attention(out_a)
    r1, r2 = shifted(p1, -1), shifted(p2, -2)

    mixed = do_mixer(
        info, my_rates, my_skips, got, local_stops, inc, back, factor, f1, f2, b1, b2
    )
    out_m = exchange(mixed.reshape(32, ROWS, 768))
    y_out, gx, gb, gc = do_unpack_mixer(out_m)
    gk, gv = do_add_kv(p0, r1, r2)
    return y_out, gx, gb, gc, att, gq, gk, gv


def solution(mesh):
    fine = Mesh(mesh.devices.reshape(-1, 4, 2, 4), ("z", "y", "core", "tp"))
    rows = P(("z", "y", "core", "tp"), None)
    return jax.shard_map(
        per_device,
        mesh=fine,
        in_specs=(rows, rows, rows, rows, P("tp"), P("tp"), rows, rows, rows, P(), rows, rows),
        out_specs=(rows,) * 8,
        check_vma=False,
    )
```

```python
import jax
import jax.numpy as jnp
from jax import lax
from jax.experimental import pallas as pl
from jax.experimental.pallas import tpu as pltpu
from jax.sharding import Mesh, PartitionSpec as P

BF = jnp.bfloat16
F32 = jnp.float32
GROUP = ("y", "core", "tp")
ROWS = 32
SUPER = 1024
BLOCK = 128
BLOCKS = SUPER // BLOCK
HEADS = 4
WIDTH = 64
CH = HEADS * WIDTH
STATE = 128
LANES = 128
SCALE = 128 ** (-0.5)
TQ = 512
TK = 512
PAD = 0
UNROLL = 2
NEG = -1e30
VMEM = 36 * 1024 * 1024
NN = (((1,), (0,)), ((), ()))
NT = (((1,), (1,)), ((), ()))
TN = (((0,), (0,)), ((), ()))


def dot(a, b, dims=NN):
    return lax.dot_general(a, b, dims, preferred_element_type=F32)


def params():
    return pltpu.CompilerParams(vmem_limit_bytes=VMEM)


def smem():
    return pl.BlockSpec(memory_space=pltpu.SMEM)


def vmem():
    return pl.BlockSpec(memory_space=pltpu.VMEM)


def places():
    for core in range(2):
        for tp in range(4):
            yield core, tp // 2, core * 4 + tp, (tp // 2) * 4 + core * 2 + tp % 2


def pack_mixer(x_ref, gy_ref, b_ref, c_ref, dt_ref, out_ref):
    for core, side, at, slot in places():
        out_ref[at, :, 0:256] = x_ref[:, slot * 256 : slot * 256 + 256]
        out_ref[at, :, 256:512] = gy_ref[:, slot * 256 : slot * 256 + 256]
        out_ref[at, :, 512:640] = b_ref[:, side * 128 : side * 128 + 128]
        out_ref[at, :, 640:768] = c_ref[:, side * 128 : side * 128 + 128]
        out_ref[at, :, 768:896] = dt_ref[...]


def pack_attention(q_ref, ga_ref, k_ref, v_ref, out_ref):
    for core, side, at, slot in places():
        out_ref[at, :, 0:128] = q_ref[:, slot * 128 : slot * 128 + 128]
        out_ref[at, :, 128:256] = ga_ref[:, slot * 128 : slot * 128 + 128]
        out_ref[at, :, 256:384] = (k_ref, v_ref)[core][:, side * 128 : side * 128 + 128]


def wide(width, place=0):
    return pl.BlockSpec((ROWS, width), lambda y: (0, y + place))


def do_pack_mixer(xs, gy, bs, cs, dts):
    return pl.pallas_call(
        pack_mixer,
        grid=(4,),
        in_specs=[wide(2048), wide(2048), wide(256), wide(256), pl.BlockSpec((ROWS, 128), lambda y: (0, 0))],
        out_specs=pl.BlockSpec((8, ROWS, 896), lambda y: (y, 0, 0)),
        out_shape=jax.ShapeDtypeStruct((32, ROWS, 896), BF),
        compiler_params=params(),
    )(xs, gy, bs, cs, dts)


def do_pack_attention(q, ga, keys, values):
    return pl.pallas_call(
        pack_attention,
        grid=(4,),
        in_specs=[wide(1024), wide(1024), wide(256), wide(256)],
        out_specs=pl.BlockSpec((8, ROWS, 384), lambda y: (y, 0, 0)),
        out_shape=jax.ShapeDtypeStruct((32, ROWS, 384), BF),
        compiler_params=params(),
    )(q, ga, keys, values)


def unpack_mixer(in_ref, y_ref, gx_ref, gb_ref, gc_ref):
    gb = [jnp.zeros((ROWS, 128), F32)] * 2
    gc = [jnp.zeros((ROWS, 128), F32)] * 2
    for core, side, at, slot in places():
        y_ref[:, slot * 256 : slot * 256 + 256] = in_ref[at, :, 0:256]
        gx_ref[:, slot * 256 : slot * 256 + 256] = in_ref[at, :, 256:512]
        gb[side] = gb[side] + in_ref[at, :, 512:640].astype(F32)
        gc[side] = gc[side] + in_ref[at, :, 640:768].astype(F32)
    gb_ref[...] = jnp.concatenate(gb, axis=1).astype(BF)
    gc_ref[...] = jnp.concatenate(gc, axis=1).astype(BF)


def do_unpack_mixer(got):
    return pl.pallas_call(
        unpack_mixer,
        grid=(4,),
        in_specs=[pl.BlockSpec((8, ROWS, 768), lambda y: (y, 0, 0))],
        out_specs=[wide(2048), wide(2048), wide(256), wide(256)],
        out_shape=[
            jax.ShapeDtypeStruct((ROWS, 8192), BF),
            jax.ShapeDtypeStruct((ROWS, 8192), BF),
            jax.ShapeDtypeStruct((ROWS, 1024), BF),
            jax.ShapeDtypeStruct((ROWS, 1024), BF),
        ],
        compiler_params=params(),
    )(got)


def unpack_attention(in_ref, att_ref, gq_ref, two_ref, one_ref, own_ref):
    refs = (two_ref, one_ref, own_ref)
    totals = {}
    for core, side, at, slot in places():
        att_ref[:, slot * 128 : slot * 128 + 128] = in_ref[at, :, 0:128]
        gq_ref[:, slot * 128 : slot * 128 + 128] = in_ref[at, :, 128:256]
        for n in range(3):
            part = in_ref[at, :, 256 + n * 128 : 384 + n * 128].astype(F32)
            where = (n, core, side)
            totals[where] = totals[where] + part if where in totals else part
    for (n, core, side), total in totals.items():
        col = core * 256 + side * 128
        refs[n][:, col : col + 128] = total.astype(refs[n].dtype)


def do_unpack_attention(got):
    return pl.pallas_call(
        unpack_attention,
        grid=(4,),
        in_specs=[pl.BlockSpec((8, ROWS, 640), lambda y: (y, 0, 0))],
        out_specs=[wide(1024), wide(1024), wide(512), wide(512), wide(512)],
        out_shape=[
            jax.ShapeDtypeStruct((ROWS, 4096), BF),
            jax.ShapeDtypeStruct((ROWS, 4096), BF),
            jax.ShapeDtypeStruct((ROWS, 2048), BF),
            jax.ShapeDtypeStruct((ROWS, 2048), BF),
            jax.ShapeDtypeStruct((ROWS, 2048), F32),
        ],
        compiler_params=params(),
    )(got)


def add_kv(own_ref, one_ref, two_ref, gk_ref, gv_ref):
    for y in range(4):
        at = slice(y * 512, y * 512 + 512)
        total = (own_ref[:, at] + one_ref[:, at].astype(F32) + two_ref[:, at].astype(F32)).astype(BF)
        gk_ref[:, y * 256 : y * 256 + 256] = total[:, 0:256]
        gv_ref[:, y * 256 : y * 256 + 256] = total[:, 256:512]


def do_add_kv(own, one, two):
    return pl.pallas_call(
        add_kv,
        in_specs=[vmem()] * 3,
        out_specs=[vmem()] * 2,
        out_shape=[jax.ShapeDtypeStruct((ROWS, 1024), BF)] * 2,
        compiler_params=params(),
    )(own, one, two)


def pack_back(att_ref, keep_ref, come_ref, out_ref):
    out_ref[:, 0:256] = att_ref[...]
    for n in range(3):
        rows = slice(n * SUPER, n * SUPER + SUPER)
        total = keep_ref[rows, :].astype(F32) + come_ref[rows, :].astype(F32)
        out_ref[:, 256 + n * 128 : 384 + n * 128] = total.astype(BF)


def do_pack_back(att, keep, come):
    return pl.pallas_call(
        pack_back,
        in_specs=[vmem()] * 3,
        out_specs=vmem(),
        out_shape=jax.ShapeDtypeStruct((SUPER, 640), BF),
        compiler_params=params(),
    )(att, keep, come)


def lane_row(values, width):
    lane = lax.broadcasted_iota(jnp.int32, (1, width * HEADS), 1)
    row = jnp.full((1, width * HEADS), values[0], F32)
    for h in range(1, HEADS):
        row = jnp.where(lane >= h * width, values[h], row)
    return row


def lower(n):
    return (
        lax.broadcasted_iota(jnp.int32, (n, n), 1) <= lax.broadcasted_iota(jnp.int32, (n, n), 0)
    ).astype(F32).astype(BF)


def upper(n):
    return (
        lax.broadcasted_iota(jnp.int32, (n, n), 0) <= lax.broadcasted_iota(jnp.int32, (n, n), 1)
    ).astype(F32).astype(BF)


def pick(first, width):
    head = lax.broadcasted_iota(jnp.int32, (128, width * HEADS), 0) - first
    lane = lax.broadcasted_iota(jnp.int32, (128, width * HEADS), 1) // width
    return (head == lane).astype(F32).astype(BF)


def channel_decay(dts, chooser, tri, rate_row, tail, entry):
    steps = dot(dts, chooser)
    cumul = dot(tri, steps.astype(BF)) * (-rate_row)
    end = cumul[BLOCK - 1 : BLOCK, :]
    row = lax.broadcasted_iota(jnp.int32, (BLOCK, CH), 0)
    weight = jnp.where(row >= tail, jnp.exp(end - cumul), 0.0)
    enter = jnp.where(row < entry, jnp.exp(cumul), 0.0)
    return steps, steps * weight, enter, end


def state_kernel(info, rates, in_ref, inc_ref, out_ref, factor_ref, sf_ref, sb_ref):
    first = info[3, 0] * HEADS
    tri = lower(BLOCK)
    chooser = pick(first, WIDTH)
    rate_row = lane_row([rates[h] for h in range(HEADS)], WIDTH)
    state = jnp.zeros((STATE, CH), F32)
    prefix = jnp.ones((1, CH), F32)
    carries = []
    pulled = []
    for j in range(BLOCKS):
        rows = slice(j * BLOCK, j * BLOCK + BLOCK)
        tail, entry, alive = info[0, j], info[1, j], info[2, j]
        _, weighted, enter, end = channel_decay(
            in_ref[rows, 768:896], chooser, tri, rate_row, tail, entry
        )
        scaled = (in_ref[rows, 0:256].astype(F32) * weighted).astype(BF)
        dcar = (in_ref[rows, 256:512].astype(F32) * enter).astype(BF)
        carry = jnp.where(alive > 0, jnp.exp(end), 0.0)
        inc_ref[j] = state
        factor_ref[j : j + 1, :] = prefix
        state = carry * state + dot(in_ref[rows, 512:640], scaled, TN)
        prefix = prefix * carry
        carries.append(carry)
        pulled.append(dot(in_ref[rows, 640:768], dcar, TN))
    high = prefix.astype(BF)
    low = (prefix - high.astype(F32)).astype(BF)
    place = lax.broadcasted_iota(jnp.int32, (16, CH), 0)
    extra = jnp.where(place == 0, high.astype(F32), jnp.where(place == 1, low.astype(F32), 0.0)).astype(BF)
    sf_ref[0:128, :] = state.astype(BF)
    sf_ref[128:144, :] = extra
    back = jnp.zeros((STATE, CH), F32)
    suffix = jnp.ones((1, CH), F32)
    for j in range(BLOCKS - 1, -1, -1):
        out_ref[j] = back
        factor_ref[8 + j : 9 + j, :] = suffix
        back = pulled[j] + carries[j] * back
        suffix = suffix * carries[j]
    sb_ref[0:128, :] = back.astype(BF)
    sb_ref[128:144, :] = extra


def do_state(info, rates, got):
    return pl.pallas_call(
        state_kernel,
        in_specs=[smem(), smem(), vmem()],
        out_specs=[vmem()] * 5,
        out_shape=[
            jax.ShapeDtypeStruct((BLOCKS, STATE, CH), F32),
            jax.ShapeDtypeStruct((BLOCKS, STATE, CH), F32),
            jax.ShapeDtypeStruct((16, CH), F32),
            jax.ShapeDtypeStruct((144, CH), BF),
            jax.ShapeDtypeStruct((144, CH), BF),
        ],
        compiler_params=params(),
    )(info, rates, got)


def joined(one_ref, two_ref):
    decay = one_ref[128:129, :].astype(F32) + one_ref[129:130, :].astype(F32)
    return one_ref[0:128, :].astype(F32) + decay * two_ref[0:128, :].astype(F32)


def mixer_kernel(
    info, rates, skips, in_ref, ends_ref, inc_ref, back_ref, factor_ref, f1, f2, b1, b2, out_ref
):
    first = info[3, 0] * HEADS
    tri = lower(BLOCK)
    triu = upper(BLOCK)
    chooser = pick(first, WIDTH)
    column_chooser = pick(first, LANES)
    head_row = lax.broadcasted_iota(jnp.int32, (8, 128), 0)
    head_at = lax.broadcasted_iota(jnp.int32, (8, 128), 1) - first
    row_chooser = ((head_row == head_at) & (head_row < HEADS)).astype(F32).astype(BF)
    rate_row = lane_row([rates[h] for h in range(HEADS)], WIDTH)
    skip_row = lane_row([skips[h] for h in range(HEADS)], WIDTH)
    entering = joined(f1, f2)
    leaving = joined(b1, b2)
    t_at = lax.broadcasted_iota(jnp.int32, (BLOCK, BLOCK), 0)
    s_at = lax.broadcasted_iota(jnp.int32, (BLOCK, BLOCK), 1)
    lane = lax.broadcasted_iota(jnp.int32, (BLOCK, CH), 1)
    owns = [(lane >= h * WIDTH) & (lane < (h + 1) * WIDTH) for h in range(HEADS)]

    def one(j, _):
        rows = pl.ds(pl.multiple_of(j * BLOCK, BLOCK), BLOCK)
        tail, entry = info[0, j], info[1, j]
        dts = in_ref[rows, 768:896]
        steps, weighted, enter, _ = channel_decay(dts, chooser, tri, rate_row, tail, entry)
        x = in_ref[rows, 0:256].astype(F32)
        gy_low = in_ref[rows, 256:512]
        gy = gy_low.astype(F32)
        b = in_ref[rows, 512:640]
        c = in_ref[rows, 640:768]
        state = (inc_ref[j] + factor_ref[pl.ds(j, 1), :] * entering).astype(BF)
        pull = (back_ref[j] + factor_ref[pl.ds(8 + j, 1), :] * leaving).astype(BF)
        columns = dot(tri, dot(dts, column_chooser).astype(BF))
        lines = dot(dot(row_chooser, dts, NT).astype(BF), triu)
        ends = ends_ref[pl.ds(j, 1), :]
        mask = (s_at <= t_at) & (t_at < ends)
        scores = dot(c, b, NT)
        driven = x * steps
        decays = []
        mixes = []
        drives = []
        for h in range(HEADS):
            gap = (columns[:, h * 128 : h * 128 + 128] - lines[h : h + 1, :]) * (-rates[h])
            decay = jnp.exp(jnp.where(mask, gap, NEG))
            decays.append(decay)
            mixes.append((decay * scores).astype(BF))
            drives.append(jnp.where(owns[h], driven, 0.0).astype(BF))
        mix = jnp.concatenate(mixes, axis=1)
        drive = jnp.concatenate(drives, axis=0)
        y = dot(mix, drive) + dot(c, state) * enter + skip_row * x
        out_ref[rows, 0:256] = y.astype(BF)
        grad_mix = dot(gy_low, drive, NT)
        grad_scores = decays[0] * grad_mix[:, 0:128]
        for h in range(1, HEADS):
            grad_scores = grad_scores + decays[h] * grad_mix[:, h * 128 : h * 128 + 128]
        grad_low = grad_scores.astype(BF)
        back = dot(mix, gy_low, TN)
        grad_drive = jnp.where(owns[0], back[0:128], 0.0)
        for h in range(1, HEADS):
            grad_drive = jnp.where(owns[h], back[h * 128 : h * 128 + 128], grad_drive)
        grad_scaled = dot(b, pull)
        gx = grad_drive * steps + grad_scaled * weighted + skip_row * gy
        out_ref[rows, 256:512] = gx.astype(BF)
        scaled = (x * weighted).astype(BF)
        dcar = (gy * enter).astype(BF)
        gb = dot(grad_low, c, TN) + dot(scaled, pull, NT)
        gc = dot(grad_low, b) + dot(dcar, state, NT)
        out_ref[rows, 512:640] = gb.astype(BF)
        out_ref[rows, 640:768] = gc.astype(BF)
        return 0

    lax.fori_loop(0, BLOCKS, one, 0, unroll=UNROLL)


def do_mixer(info, rates, skips, got, ends, inc, back, factor, f1, f2, b1, b2):
    return pl.pallas_call(
        mixer_kernel,
        in_specs=[smem()] * 3 + [vmem()] * 9,
        out_specs=vmem(),
        out_shape=jax.ShapeDtypeStruct((SUPER, 768), BF),
        compiler_params=params(),
    )(info, rates, skips, got, ends, inc, back, factor, f1, f2, b1, b2)


def attention_kernel(
    core, starts, in_ref, own1, own2, oth0, oth1, oth2, start_ref, out_ref, keep_ref, send_ref,
    k_ref, v_ref, kt_ref, vt_ref, near_ref, far_ref, peak_ref, gk_ref, gv_ref
):
    count = SUPER // TQ
    lowest = starts[0] - TK + 1
    gk_ref[...] = jnp.zeros_like(gk_ref)
    gv_ref[...] = jnp.zeros_like(gv_ref)
    for n in range(3):
        rows = slice(PAD + n * SUPER, PAD + n * SUPER + SUPER)
        own = (own2, own1, in_ref.at[:, 256:384])[n]
        other = (oth2, oth1, oth0)[n]

        @pl.when((lowest < (n + 1) * SUPER) & (core[0] == 0))
        def _():
            k_ref[rows, :] = own[...]
            v_ref[rows, :] = other[...]

        @pl.when((lowest < (n + 1) * SUPER) & (core[0] != 0))
        def _():
            k_ref[rows, :] = other[...]
            v_ref[rows, :] = own[...]

        @pl.when(lowest < (n + 1) * SUPER)
        def _():
            kt_ref[:, rows] = k_ref[rows, :].T
            vt_ref[:, rows] = v_ref[rows, :].T

    def tile_sum(p):
        return jnp.sum(p.reshape(p.shape[0] // 8, 8, TQ), axis=0)

    at = lax.broadcasted_iota(jnp.int32, (TQ, TQ), 0)
    here = lax.broadcasted_iota(jnp.int32, (TQ, TQ), 1)
    far_at = lax.broadcasted_iota(jnp.int32, (TK, TQ), 0)
    q_rows = [slice(i * TQ, i * TQ + TQ) for i in range(count)]
    diag = [2 * SUPER + i * TQ for i in range(count)]
    near = [slice(PAD + diag[i], PAD + diag[i] + TQ) for i in range(count)]
    begins = [start_ref[i : i + 1, :] for i in range(count)]
    many = [(jnp.maximum(diag[i] - starts[i * TQ], 0) + TK - 1) // TK for i in range(count)]

    carries = []
    for i in range(count):
        q = in_ref[q_rows[i], 0:128]
        s = dot(k_ref[near[i], :], q, NT)
        s = jnp.where((at + diag[i] >= begins[i]) & (at <= here), s, NEG)
        peak = jnp.max(s, axis=0, keepdims=True)
        p = jnp.exp((s - peak) * SCALE)
        near_ref[i] = p
        peak_ref[i, 4:5, :] = peak
        carries.append((peak, tile_sum(p), dot(vt_ref[:, near[i]], p.astype(BF))))

    for i in range(count):
        q = in_ref[q_rows[i], 0:128]

        def forward(t, carry):
            peak, total, att = carry
            base = diag[i] - TK * (t + 1)
            rows = pl.ds(pl.multiple_of(PAD + base, TQ), TK)
            s = dot(k_ref[rows, :], q, NT)
            s = jnp.where(far_at >= begins[i] - base, s, NEG)
            top = jnp.maximum(peak, jnp.max(s, axis=0, keepdims=True))
            alpha = jnp.exp((peak - top) * SCALE)
            p = jnp.exp((s - top) * SCALE)
            far_ref[i, t] = p
            peak_ref[i, pl.ds(t, 1), :] = top
            att = att * alpha + dot(vt_ref[:, rows], p.astype(BF))
            return top, total * alpha + tile_sum(p), att

        carries[i] = lax.fori_loop(0, many[i], forward, carries[i])

    rest = []
    for i in range(count):
        peak, total, att = carries[i]
        q = in_ref[q_rows[i], 0:128]
        ga = in_ref[q_rows[i], 128:256]
        inverse = 1.0 / jnp.sum(total, axis=0, keepdims=True)
        att = (att * inverse).astype(BF)
        out_ref[q_rows[i], 0:128] = att.T
        delta = jnp.sum(ga.T.astype(F32) * att.astype(F32), axis=0, keepdims=True)
        probs = near_ref[i] * (jnp.exp((peak_ref[i, 4:5, :] - peak) * SCALE) * inverse)
        ds = (probs * (dot(v_ref[near[i], :], ga, NT) - delta)).astype(BF)
        gk_ref[near[i], :] += dot(ds, q)
        gv_ref[near[i], :] += dot(probs.astype(BF), ga)
        rest.append((peak, inverse, delta, dot(kt_ref[:, near[i]], ds)))

    for i in range(count):
        peak, inverse, delta, gq = rest[i]
        q = in_ref[q_rows[i], 0:128]
        ga = in_ref[q_rows[i], 128:256]

        def backward(t, gq):
            rows = pl.ds(pl.multiple_of(PAD + diag[i] - TK * (t + 1), TQ), TK)
            factor = jnp.exp((peak_ref[i, pl.ds(t, 1), :] - peak) * SCALE) * inverse
            probs = far_ref[i, t] * factor
            ds = (probs * (dot(v_ref[rows, :], ga, NT) - delta)).astype(BF)
            gk_ref[rows, :] += dot(ds, q)
            gv_ref[rows, :] += dot(probs.astype(BF), ga)
            return gq + dot(kt_ref[:, rows], ds)

        gq = lax.fori_loop(0, many[i], backward, gq)
        out_ref[q_rows[i], 128:256] = (gq * SCALE).astype(BF).T

    def store(k_out, v_out):
        k_out[...] = (gk_ref[PAD:, :] * SCALE).astype(BF)
        v_out[...] = gv_ref[PAD:, :].astype(BF)

    @pl.when(core[0] == 0)
    def _():
        store(keep_ref, send_ref)

    @pl.when(core[0] != 0)
    def _():
        store(send_ref, keep_ref)


def do_attention(core, starts, got, own1, own2, oth0, oth1, oth2):
    span = PAD + 3 * SUPER
    count = SUPER // TQ
    return pl.pallas_call(
        attention_kernel,
        in_specs=[smem(), smem()] + [vmem()] * 7,
        out_specs=[vmem()] * 3,
        out_shape=[
            jax.ShapeDtypeStruct((SUPER, 256), BF),
            jax.ShapeDtypeStruct((3 * SUPER, 128), BF),
            jax.ShapeDtypeStruct((3 * SUPER, 128), BF),
        ],
        scratch_shapes=[
            pltpu.VMEM((span, 128), BF),
            pltpu.VMEM((span, 128), BF),
            pltpu.VMEM((128, span), BF),
            pltpu.VMEM((128, span), BF),
            pltpu.VMEM((count, TQ, TQ), F32),
            pltpu.VMEM((count, 4, TK, TQ), F32),
            pltpu.VMEM((count, 8, TQ), F32),
            pltpu.VMEM((span, 128), F32),
            pltpu.VMEM((span, 128), F32),
        ],
        compiler_params=params(),
    )(core, starts, got, own1, own2, oth0, oth1, oth2, starts.reshape(SUPER // TQ, TQ))


def shifted(block, distance):
    count = lax.axis_size("z")
    route = [(i, i + distance) for i in range(count) if 0 <= i + distance < count]
    return lax.ppermute(block, "z", route)


def exchange(block):
    return lax.all_to_all(block, GROUP, split_axis=0, concat_axis=0, tiled=True)


def swapped(block):
    return lax.ppermute(block, "core", [(0, 1), (1, 0)])


def per_device(xs, dts, bs, cs, rates, skips, queries, keys, values, lengths, grad_y, grad_attn):
    z, y, core, tp = (lax.axis_index(a) for a in ("z", "y", "core", "tp"))
    inside = (tp // 2) * 4 + core * 2 + tp % 2
    device = y * 8 + inside

    packed_a = do_pack_attention(queries, grad_attn, keys, values)
    packed_a, xs, rates = lax.optimization_barrier((packed_a, xs, rates))
    side = lax.axis_size("tp")
    both = lax.ppermute(
        jnp.stack([rates, skips]),
        ("y", "tp"),
        [(a * side + b, b * side + a) for a in range(side) for b in range(side)],
    )
    packed_m = do_pack_mixer(xs, grad_y, bs, cs, dts)
    mine = lax.dynamic_slice_in_dim(both, inside * HEADS, HEADS, 1)
    my_rates, my_skips = mine[0], mine[1]

    ends = jnp.cumsum(lengths)
    begins = ends - lengths
    base = z * SUPER
    positions = base + jnp.arange(SUPER, dtype=jnp.int32)
    starts = jnp.max(jnp.where(begins[None, :] <= positions[:, None], begins[None, :], 0), axis=1)
    stops = jnp.min(
        jnp.where(ends[None, :] > positions[:, None], ends[None, :], SUPER * 8), axis=1
    )
    block_at = base + jnp.arange(BLOCKS, dtype=jnp.int32) * BLOCK
    last_start = starts[BLOCK - 1 :: BLOCK]
    prior_stop = jnp.min(
        jnp.where(ends[None, :] >= block_at[:, None], ends[None, :], SUPER * 8), axis=1
    )
    entry = jnp.where(block_at > 0, prior_stop - block_at, 0)
    info = jnp.stack(
        [
            last_start - block_at,
            entry,
            (last_start < block_at).astype(jnp.int32),
            jnp.full((BLOCKS,), device, jnp.int32),
        ]
    )
    local_stops = (stops.reshape(BLOCKS, BLOCK) - block_at[:, None]).astype(jnp.int32)

    got_a = exchange(packed_a)
    packed_m, got_a = lax.optimization_barrier((packed_m, got_a))
    got_a = got_a.reshape(SUPER, 384)
    own0 = got_a[:, 256:384]
    own1, own2 = shifted(own0, 1), shifted(own0, 2)
    got = exchange(packed_m)
    att, keep, send = do_attention(
        jnp.full((1,), core, jnp.int32),
        (starts - (base - 2 * SUPER)).astype(jnp.int32),
        got_a, own1, own2, swapped(own0), swapped(own1), swapped(own2),
    )
    send, got = lax.optimization_barrier((send, got))
    got = got.reshape(SUPER, 896)
    packed_b = do_pack_back(att, keep, swapped(send))
    out_a = exchange(packed_b.reshape(32, ROWS, 640))

    inc, back, factor, send_f, send_b = do_state(info, my_rates, got)
    f1, f2 = shifted(send_f, 1), shifted(send_f, 2)
    b1, b2 = shifted(send_b, -1), shifted(send_b, -2)
    mixed = do_mixer(
        info, my_rates, my_skips, got, local_stops, inc, back, factor, f1, f2, b1, b2
    )
    mixed, out_a = lax.optimization_barrier((mixed, out_a))
    out_m = exchange(mixed.reshape(32, ROWS, 768))
    att, gq, p2, p1, p0 = do_unpack_attention(out_a)
    r1, r2 = shifted(p1, -1), shifted(p2, -2)
    gk, gv = do_add_kv(p0, r1, r2)
    y_out, gx, gb, gc = do_unpack_mixer(out_m)
    return y_out, gx, gb, gc, att, gq, gk, gv


def solution(mesh):
    fine = Mesh(mesh.devices.reshape(-1, 4, 2, 4), ("z", "y", "core", "tp"))
    rows = P(("z", "y", "core", "tp"), None)
    return jax.shard_map(
        per_device,
        mesh=fine,
        in_specs=(rows, rows, rows, rows, P("tp"), P("tp"), rows, rows, rows, P(), rows, rows),
        out_specs=(rows,) * 8,
        check_vma=False,
    )
```

```python
import jax
import jax.numpy as jnp
from jax import lax
from jax.experimental import pallas as pl
from jax.experimental.pallas import tpu as pltpu
from jax.sharding import Mesh, PartitionSpec as P

BF = jnp.bfloat16
F32 = jnp.float32
GROUP = ("y", "core", "tp")
ROWS = 32
SUPER = 1024
BLOCK = 128
BLOCKS = SUPER // BLOCK
HEADS = 4
WIDTH = 64
CH = HEADS * WIDTH
STATE = 128
LANES = 128
SCALE = 128 ** (-0.5)
TQ = 512
TK = 512
UNROLL = 2
ATT = 5
NEG = -1e30
NN = (((1,), (0,)), ((), ()))
NT = (((1,), (1,)), ((), ()))
TN = (((0,), (0,)), ((), ()))


def dot(a, b, dims=NN):
    return lax.dot_general(a, b, dims, preferred_element_type=F32)


def params(mib=8):
    return pltpu.CompilerParams(vmem_limit_bytes=mib * 1024 * 1024)


def in_hbm(*arrays):
    return [pltpu.with_memory_space_constraint(a, pltpu.HBM) for a in arrays]


def in_vmem(*arrays):
    return [pltpu.with_memory_space_constraint(a, pltpu.VMEM) for a in arrays]


def cost(micros):
    return pl.CostEstimate(flops=int(micros * 10**9), bytes_accessed=10**6, transcendentals=0)


def smem():
    return pl.BlockSpec(memory_space=pltpu.SMEM)


def vmem():
    return pl.BlockSpec(memory_space=pltpu.VMEM)


def places():
    for core in range(2):
        for tp in range(4):
            yield core, tp // 2, core * 4 + tp, (tp // 2) * 4 + core * 2 + tp % 2


def pack_mixer(x_ref, gy_ref, b_ref, c_ref, dt_ref, out_ref):
    for core, side, at, slot in places():
        out_ref[at, :, 0:256] = x_ref[:, slot * 256 : slot * 256 + 256]
        out_ref[at, :, 256:512] = gy_ref[:, slot * 256 : slot * 256 + 256]
        out_ref[at, :, 512:640] = b_ref[:, side * 128 : side * 128 + 128]
        out_ref[at, :, 640:768] = c_ref[:, side * 128 : side * 128 + 128]
        out_ref[at, :, 768:896] = dt_ref[...]


def pack_attention(q_ref, ga_ref, k_ref, v_ref, out_ref):
    for core, side, at, slot in places():
        out_ref[at, :, 0:128] = q_ref[:, slot * 128 : slot * 128 + 128]
        out_ref[at, :, 128:256] = ga_ref[:, slot * 128 : slot * 128 + 128]
        out_ref[at, :, 256:384] = (k_ref, v_ref)[core][:, side * 128 : side * 128 + 128]


def wide(width, place=0):
    return pl.BlockSpec((ROWS, width), lambda y: (0, y + place))


def do_pack_mixer(xs, gy, bs, cs, dts):
    return pl.pallas_call(
        pack_mixer,
        grid=(4,),
        in_specs=[wide(2048), wide(2048), wide(256), wide(256), pl.BlockSpec((ROWS, 128), lambda y: (0, 0))],
        out_specs=pl.BlockSpec((8, ROWS, 896), lambda y: (y, 0, 0)),
        out_shape=pltpu.HBM((32, ROWS, 896), BF),
        compiler_params=params(),
    )(*in_hbm(xs, gy, bs, cs, dts))


def do_pack_attention(q, ga, keys, values):
    return pl.pallas_call(
        pack_attention,
        grid=(4,),
        in_specs=[wide(1024), wide(1024), wide(256), wide(256)],
        out_specs=pl.BlockSpec((8, ROWS, 384), lambda y: (y, 0, 0)),
        out_shape=pltpu.HBM((32, ROWS, 384), BF),
        compiler_params=params(),
    )(*in_hbm(q, ga, keys, values))


def unpack_mixer(in_ref, y_ref, gx_ref, gb_ref, gc_ref):
    gb = [jnp.zeros((ROWS, 128), F32)] * 2
    gc = [jnp.zeros((ROWS, 128), F32)] * 2
    for core, side, at, slot in places():
        y_ref[:, slot * 256 : slot * 256 + 256] = in_ref[at, :, 0:256]
        gx_ref[:, slot * 256 : slot * 256 + 256] = in_ref[at, :, 256:512]
        gb[side] = gb[side] + in_ref[at, :, 512:640].astype(F32)
        gc[side] = gc[side] + in_ref[at, :, 640:768].astype(F32)
    gb_ref[...] = jnp.concatenate(gb, axis=1).astype(BF)
    gc_ref[...] = jnp.concatenate(gc, axis=1).astype(BF)


def do_unpack_mixer(got):
    return pl.pallas_call(
        unpack_mixer,
        grid=(4,),
        in_specs=[pl.BlockSpec((8, ROWS, 768), lambda y: (y, 0, 0))],
        out_specs=[wide(2048), wide(2048), wide(256), wide(256)],
        out_shape=[
            jax.ShapeDtypeStruct((ROWS, 8192), BF),
            jax.ShapeDtypeStruct((ROWS, 8192), BF),
            jax.ShapeDtypeStruct((ROWS, 1024), BF),
            jax.ShapeDtypeStruct((ROWS, 1024), BF),
        ],
        compiler_params=params(),
    )(got)


def unpack_attention(in_ref, att_ref, gq_ref, two_ref, one_ref, own_ref):
    refs = (two_ref, one_ref, own_ref)
    totals = {}
    for core, side, at, slot in places():
        att_ref[:, slot * 128 : slot * 128 + 128] = in_ref[at, :, 0:128]
        gq_ref[:, slot * 128 : slot * 128 + 128] = in_ref[at, :, 128:256]
        for n in range(3):
            part = in_ref[at, :, 256 + n * 128 : 384 + n * 128].astype(F32)
            where = (n, core, side)
            totals[where] = totals[where] + part if where in totals else part
    for (n, core, side), total in totals.items():
        col = core * 256 + side * 128
        refs[n][:, col : col + 128] = total.astype(refs[n].dtype)


def do_unpack_attention(got):
    return pl.pallas_call(
        unpack_attention,
        grid=(4,),
        in_specs=[pl.BlockSpec((8, ROWS, 640), lambda y: (y, 0, 0))],
        out_specs=[wide(1024), wide(1024), wide(512), wide(512), wide(512)],
        out_shape=[
            jax.ShapeDtypeStruct((ROWS, 4096), BF),
            jax.ShapeDtypeStruct((ROWS, 4096), BF),
            jax.ShapeDtypeStruct((ROWS, 2048), BF),
            jax.ShapeDtypeStruct((ROWS, 2048), BF),
            jax.ShapeDtypeStruct((ROWS, 2048), F32),
        ],
        compiler_params=params(),
    )(got)


def add_kv(own_ref, one_ref, two_ref, gk_ref, gv_ref):
    for y in range(4):
        at = slice(y * 512, y * 512 + 512)
        total = (own_ref[:, at] + one_ref[:, at].astype(F32) + two_ref[:, at].astype(F32)).astype(BF)
        gk_ref[:, y * 256 : y * 256 + 256] = total[:, 0:256]
        gv_ref[:, y * 256 : y * 256 + 256] = total[:, 256:512]


def do_add_kv(own, one, two):
    return pl.pallas_call(
        add_kv,
        in_specs=[vmem()] * 3,
        out_specs=[vmem()] * 2,
        out_shape=[jax.ShapeDtypeStruct((ROWS, 1024), BF)] * 2,
        compiler_params=params(),
    )(own, one, two)


def pack_back(att_ref, keep_ref, come_ref, out_ref):
    out_ref[:, 0:256] = att_ref[...]
    for n in range(3):
        rows = slice(n * SUPER, n * SUPER + SUPER)
        total = keep_ref[rows, :].astype(F32) + come_ref[rows, :].astype(F32)
        out_ref[:, 256 + n * 128 : 384 + n * 128] = total.astype(BF)


def do_pack_back(att, keep, come):
    return pl.pallas_call(
        pack_back,
        in_specs=[vmem()] * 3,
        out_specs=vmem(),
        out_shape=pltpu.HBM((SUPER, 640), BF),
        compiler_params=params(),
    )(*in_hbm(att, keep), come)


def lane_row(values, width):
    lane = lax.broadcasted_iota(jnp.int32, (1, width * HEADS), 1)
    row = jnp.full((1, width * HEADS), values[0], F32)
    for h in range(1, HEADS):
        row = jnp.where(lane >= h * width, values[h], row)
    return row


def lower(n):
    return (
        lax.broadcasted_iota(jnp.int32, (n, n), 1) <= lax.broadcasted_iota(jnp.int32, (n, n), 0)
    ).astype(F32).astype(BF)


def upper(n):
    return (
        lax.broadcasted_iota(jnp.int32, (n, n), 0) <= lax.broadcasted_iota(jnp.int32, (n, n), 1)
    ).astype(F32).astype(BF)


def pick(first, width):
    head = lax.broadcasted_iota(jnp.int32, (128, width * HEADS), 0) - first
    lane = lax.broadcasted_iota(jnp.int32, (128, width * HEADS), 1) // width
    return (head == lane).astype(F32).astype(BF)


def channel_decay(dts, chooser, tri, rate_row, tail, entry):
    steps = dot(dts, chooser)
    cumul = dot(tri, steps.astype(BF)) * (-rate_row)
    end = cumul[BLOCK - 1 : BLOCK, :]
    row = lax.broadcasted_iota(jnp.int32, (BLOCK, CH), 0)
    weight = jnp.where(row >= tail, jnp.exp(end - cumul), 0.0)
    enter = jnp.where(row < entry, jnp.exp(cumul), 0.0)
    return steps, steps * weight, enter, end


def state_kernel(
    info, rates, in_ref, inc_ref, out_ref, factor_ref, sf_ref, sb_ref, low_ref, full_ref
):
    first = info[3, 0] * HEADS
    tri = lower(BLOCK)
    chooser = pick(first, WIDTH)
    rate_row = lane_row([rates[h] for h in range(HEADS)], WIDTH)
    state = jnp.zeros((STATE, CH), F32)
    prefix = jnp.ones((1, CH), F32)
    carries = []
    pulled = []
    for j in range(BLOCKS):
        rows = slice(j * BLOCK, j * BLOCK + BLOCK)
        tail, entry, alive = info[0, j], info[1, j], info[2, j]
        _, weighted, enter, end = channel_decay(
            in_ref[rows, 768:896], chooser, tri, rate_row, tail, entry
        )
        scaled = (in_ref[rows, 0:256].astype(F32) * weighted).astype(BF)
        dcar = (in_ref[rows, 256:512].astype(F32) * enter).astype(BF)
        low_ref[rows, 0:256] = scaled
        low_ref[rows, 256:512] = dcar
        full_ref[rows, 0:256] = weighted
        full_ref[rows, 256:512] = enter
        carry = jnp.where(alive > 0, jnp.exp(end), 0.0)
        inc_ref[j] = state
        factor_ref[j : j + 1, :] = prefix
        state = carry * state + dot(in_ref[rows, 512:640], scaled, TN)
        prefix = prefix * carry
        carries.append(carry)
        pulled.append(dot(in_ref[rows, 640:768], dcar, TN))
    high = prefix.astype(BF)
    low = (prefix - high.astype(F32)).astype(BF)
    place = lax.broadcasted_iota(jnp.int32, (16, CH), 0)
    extra = jnp.where(place == 0, high.astype(F32), jnp.where(place == 1, low.astype(F32), 0.0)).astype(BF)
    sf_ref[0:128, :] = state.astype(BF)
    sf_ref[128:144, :] = extra
    back = jnp.zeros((STATE, CH), F32)
    suffix = jnp.ones((1, CH), F32)
    for j in range(BLOCKS - 1, -1, -1):
        out_ref[j] = back
        factor_ref[8 + j : 9 + j, :] = suffix
        back = pulled[j] + carries[j] * back
        suffix = suffix * carries[j]
    sb_ref[0:128, :] = back.astype(BF)
    sb_ref[128:144, :] = extra


def do_state(info, rates, got):
    return pl.pallas_call(
        state_kernel,
        in_specs=[smem(), smem(), vmem()],
        out_specs=[vmem()] * 7,
        out_shape=[
            pltpu.VMEM((BLOCKS, STATE, CH), F32),
            pltpu.VMEM((BLOCKS, STATE, CH), F32),
            pltpu.VMEM((16, CH), F32),
            jax.ShapeDtypeStruct((144, CH), BF),
            jax.ShapeDtypeStruct((144, CH), BF),
            pltpu.VMEM((SUPER, 512), BF),
            pltpu.VMEM((SUPER, 512), F32),
        ],
        compiler_params=params(12),
        cost_estimate=cost(3),
    )(info, rates, *in_vmem(got))


def joined(one_ref, two_ref):
    decay = one_ref[128:129, :].astype(F32) + one_ref[129:130, :].astype(F32)
    return one_ref[0:128, :].astype(F32) + decay * two_ref[0:128, :].astype(F32)


def inner_kernel(info, rates, skips, in_ref, ends_ref, out_ref):
    first = info[3, 0] * HEADS
    tri = lower(BLOCK)
    triu = upper(BLOCK)
    chooser = pick(first, WIDTH)
    column_chooser = pick(first, LANES)
    head_row = lax.broadcasted_iota(jnp.int32, (8, 128), 0)
    head_at = lax.broadcasted_iota(jnp.int32, (8, 128), 1) - first
    row_chooser = ((head_row == head_at) & (head_row < HEADS)).astype(F32).astype(BF)
    skip_row = lane_row([skips[h] for h in range(HEADS)], WIDTH)
    t_at = lax.broadcasted_iota(jnp.int32, (BLOCK, BLOCK), 0)
    s_at = lax.broadcasted_iota(jnp.int32, (BLOCK, BLOCK), 1)
    lane = lax.broadcasted_iota(jnp.int32, (BLOCK, CH), 1)
    owns = [(lane >= h * WIDTH) & (lane < (h + 1) * WIDTH) for h in range(HEADS)]

    def one(j, _):
        rows = pl.ds(pl.multiple_of(j * BLOCK, BLOCK), BLOCK)
        dts = in_ref[rows, 768:896]
        steps = dot(dts, chooser)
        x = in_ref[rows, 0:256].astype(F32)
        gy_low = in_ref[rows, 256:512]
        b = in_ref[rows, 512:640]
        c = in_ref[rows, 640:768]
        columns = dot(tri, dot(dts, column_chooser).astype(BF))
        lines = dot(dot(row_chooser, dts, NT).astype(BF), triu)
        ends = ends_ref[pl.ds(j, 1), :]
        mask = (s_at <= t_at) & (t_at < ends)
        scores = dot(c, b, NT)
        driven = x * steps
        decays = []
        mixes = []
        drives = []
        for h in range(HEADS):
            gap = (columns[:, h * 128 : h * 128 + 128] - lines[h : h + 1, :]) * (-rates[h])
            decay = jnp.exp(jnp.where(mask, gap, NEG))
            decays.append(decay)
            mixes.append((decay * scores).astype(BF))
            drives.append(jnp.where(owns[h], driven, 0.0).astype(BF))
        mix = jnp.concatenate(mixes, axis=1)
        drive = jnp.concatenate(drives, axis=0)
        out_ref[rows, 0:256] = dot(mix, drive) + skip_row * x
        grad_mix = dot(gy_low, drive, NT)
        grad_scores = decays[0] * grad_mix[:, 0:128]
        for h in range(1, HEADS):
            grad_scores = grad_scores + decays[h] * grad_mix[:, h * 128 : h * 128 + 128]
        grad_low = grad_scores.astype(BF)
        back = dot(mix, gy_low, TN)
        grad_drive = jnp.where(owns[0], back[0:128], 0.0)
        for h in range(1, HEADS):
            grad_drive = jnp.where(owns[h], back[h * 128 : h * 128 + 128], grad_drive)
        out_ref[rows, 256:512] = grad_drive * steps + skip_row * gy_low.astype(F32)
        out_ref[rows, 512:640] = dot(grad_low, c, TN)
        out_ref[rows, 640:768] = dot(grad_low, b)
        return 0

    lax.fori_loop(0, BLOCKS, one, 0, unroll=UNROLL)


def do_inner(info, rates, skips, got, ends):
    return pl.pallas_call(
        inner_kernel,
        in_specs=[smem()] * 3 + [vmem()] * 2,
        out_specs=vmem(),
        out_shape=pltpu.VMEM((SUPER, 768), F32),
        compiler_params=params(12),
        cost_estimate=cost(8),
    )(info, rates, skips, *in_vmem(got), ends)


def outer_kernel(
    in_ref, part_ref, low_ref, full_ref, inc_ref, back_ref, factor_ref, f1, f2, b1, b2, out_ref
):
    entering = joined(f1, f2)
    leaving = joined(b1, b2)
    for j in range(BLOCKS):
        rows = slice(j * BLOCK, j * BLOCK + BLOCK)
        b = in_ref[rows, 512:640]
        c = in_ref[rows, 640:768]
        state = (inc_ref[j] + factor_ref[j : j + 1, :] * entering).astype(BF)
        pull = (back_ref[j] + factor_ref[8 + j : 9 + j, :] * leaving).astype(BF)
        y = part_ref[rows, 0:256] + dot(c, state) * full_ref[rows, 256:512]
        gx = part_ref[rows, 256:512] + dot(b, pull) * full_ref[rows, 0:256]
        gb = part_ref[rows, 512:640] + dot(low_ref[rows, 0:256], pull, NT)
        gc = part_ref[rows, 640:768] + dot(low_ref[rows, 256:512], state, NT)
        out_ref[rows, 0:256] = y.astype(BF)
        out_ref[rows, 256:512] = gx.astype(BF)
        out_ref[rows, 512:640] = gb.astype(BF)
        out_ref[rows, 640:768] = gc.astype(BF)


def do_outer(*operands):
    return pl.pallas_call(
        outer_kernel,
        in_specs=[vmem()] * 11,
        out_specs=vmem(),
        out_shape=pltpu.HBM((SUPER, 768), BF),
        compiler_params=params(16),
        cost_estimate=cost(2),
    )(*in_vmem(*operands))


def attention_kernel(
    core, starts, in_ref, own0, own1, own2, oth0, oth1, oth2, start_ref, out_ref, keep_ref, send_ref,
    k_ref, v_ref, kt_ref, vt_ref, near_ref, far_ref, peak_ref, gk_ref, gv_ref, sems
):
    count = SUPER // TQ
    lowest = starts[0] - TK + 1
    places_of = [slice(n * SUPER, n * SUPER + SUPER) for n in range(3)]
    owns = (own2, own1, own0)
    others = (oth2, oth1, oth0)

    def moves(n, first):
        mine, theirs = (owns[n], others[n]) if first else (others[n], owns[n])
        return (
            pltpu.make_async_copy(mine, k_ref.at[places_of[n], :], sems.at[2 * n]),
            pltpu.make_async_copy(theirs, v_ref.at[places_of[n], :], sems.at[2 * n + 1]),
        )

    def on_core(n, first, act):
        @pl.when((lowest < (n + 1) * SUPER) & ((core[0] == 0) == first))
        def _():
            for move in moves(n, first):
                act(move)

    for n in (2, 1, 0):
        on_core(n, True, lambda move: move.start())
        on_core(n, False, lambda move: move.start())
    gk_ref[...] = jnp.zeros_like(gk_ref)
    gv_ref[...] = jnp.zeros_like(gv_ref)
    for n in (2, 1, 0):
        on_core(n, True, lambda move: move.wait())
        on_core(n, False, lambda move: move.wait())

        @pl.when(lowest < (n + 1) * SUPER)
        def _():
            kt_ref[:, places_of[n]] = k_ref[places_of[n], :].T
            vt_ref[:, places_of[n]] = v_ref[places_of[n], :].T

    def tile_sum(p):
        return jnp.sum(p.reshape(p.shape[0] // 8, 8, TQ), axis=0)

    at = lax.broadcasted_iota(jnp.int32, (TQ, TQ), 0)
    here = lax.broadcasted_iota(jnp.int32, (TQ, TQ), 1)
    far_at = lax.broadcasted_iota(jnp.int32, (TK, TQ), 0)
    q_rows = [slice(i * TQ, i * TQ + TQ) for i in range(count)]
    diag = [2 * SUPER + i * TQ for i in range(count)]
    near = [slice(diag[i], diag[i] + TQ) for i in range(count)]
    begins = [start_ref[i : i + 1, :] for i in range(count)]
    many = [(jnp.maximum(diag[i] - starts[i * TQ], 0) + TK - 1) // TK for i in range(count)]

    carries = []
    for i in range(count):
        q = in_ref[q_rows[i], 0:128]
        s = dot(k_ref[near[i], :], q, NT)
        s = jnp.where((at + diag[i] >= begins[i]) & (at <= here), s, NEG)
        peak = jnp.max(s, axis=0, keepdims=True)
        p = jnp.exp((s - peak) * SCALE)
        near_ref[i] = p
        peak_ref[i, 4:5, :] = peak
        carries.append((peak, tile_sum(p), dot(vt_ref[:, near[i]], p.astype(BF))))

    for i in range(count):
        q = in_ref[q_rows[i], 0:128]

        def forward(t, carry):
            peak, total, att = carry
            base = diag[i] - TK * (t + 1)
            rows = pl.ds(pl.multiple_of(base, TQ), TK)
            s = dot(k_ref[rows, :], q, NT)
            s = jnp.where(far_at >= begins[i] - base, s, NEG)
            top = jnp.maximum(peak, jnp.max(s, axis=0, keepdims=True))
            alpha = jnp.exp((peak - top) * SCALE)
            p = jnp.exp((s - top) * SCALE)
            far_ref[i, t] = p
            peak_ref[i, pl.ds(t, 1), :] = top
            att = att * alpha + dot(vt_ref[:, rows], p.astype(BF))
            return top, total * alpha + tile_sum(p), att

        carries[i] = lax.fori_loop(0, many[i], forward, carries[i])

    rest = []
    for i in range(count):
        peak, total, att = carries[i]
        q = in_ref[q_rows[i], 0:128]
        ga = in_ref[q_rows[i], 128:256]
        inverse = 1.0 / jnp.sum(total, axis=0, keepdims=True)
        att = (att * inverse).astype(BF)
        out_ref[q_rows[i], 0:128] = att.T
        delta = jnp.sum(ga.T.astype(F32) * att.astype(F32), axis=0, keepdims=True)
        probs = near_ref[i] * (jnp.exp((peak_ref[i, 4:5, :] - peak) * SCALE) * inverse)
        ds = (probs * (dot(v_ref[near[i], :], ga, NT) - delta)).astype(BF)
        gk_ref[near[i], :] += dot(ds, q)
        gv_ref[near[i], :] += dot(probs.astype(BF), ga)
        rest.append((peak, inverse, delta, dot(kt_ref[:, near[i]], ds)))

    for i in range(count):
        peak, inverse, delta, gq = rest[i]
        q = in_ref[q_rows[i], 0:128]
        ga = in_ref[q_rows[i], 128:256]

        def backward(t, gq):
            rows = pl.ds(pl.multiple_of(diag[i] - TK * (t + 1), TQ), TK)
            factor = jnp.exp((peak_ref[i, pl.ds(t, 1), :] - peak) * SCALE) * inverse
            probs = far_ref[i, t] * factor
            ds = (probs * (dot(v_ref[rows, :], ga, NT) - delta)).astype(BF)
            gk_ref[rows, :] += dot(ds, q)
            gv_ref[rows, :] += dot(probs.astype(BF), ga)
            return gq + dot(kt_ref[:, rows], ds)

        gq = lax.fori_loop(0, many[i], backward, gq)
        out_ref[q_rows[i], 128:256] = (gq * SCALE).astype(BF).T

    def store(k_out, v_out):
        k_out[...] = (gk_ref[...] * SCALE).astype(BF)
        v_out[...] = gv_ref[...].astype(BF)

    @pl.when(core[0] == 0)
    def _():
        store(keep_ref, send_ref)

    @pl.when(core[0] != 0)
    def _():
        store(send_ref, keep_ref)


def do_attention(core, starts, *moved):
    span = 3 * SUPER
    count = SUPER // TQ
    return pl.pallas_call(
        attention_kernel,
        in_specs=[smem()] * 2 + [vmem()] + [pl.BlockSpec(memory_space=pl.ANY)] * 6 + [vmem()],
        out_specs=[vmem()] * 3,
        out_shape=[
            pltpu.HBM((SUPER, 256), BF),
            pltpu.HBM((3 * SUPER, 128), BF),
            pltpu.HBM((3 * SUPER, 128), BF),
        ],
        scratch_shapes=[
            pltpu.VMEM((span, 128), BF),
            pltpu.VMEM((span, 128), BF),
            pltpu.VMEM((128, span), BF),
            pltpu.VMEM((128, span), BF),
            pltpu.VMEM((count, TQ, TQ), F32),
            pltpu.VMEM((count, 4, TK, TQ), F32),
            pltpu.VMEM((count, 8, TQ), F32),
            pltpu.VMEM((span, 128), F32),
            pltpu.VMEM((span, 128), F32),
            pltpu.SemaphoreType.DMA((6,)),
        ],
        compiler_params=params(28),
        cost_estimate=cost(ATT),
    )(core, starts, *moved, starts.reshape(SUPER // TQ, TQ))


def shifted(block, distance):
    count = lax.axis_size("z")
    route = [(i, i + distance) for i in range(count) if 0 <= i + distance < count]
    return lax.ppermute(block, "z", route)


def exchange(block):
    return lax.all_to_all(block, GROUP, split_axis=0, concat_axis=0, tiled=True)


def swapped(block):
    return lax.ppermute(block, "core", [(0, 1), (1, 0)])


def per_device(xs, dts, bs, cs, rates, skips, queries, keys, values, lengths, grad_y, grad_attn):
    z, y, core, tp = (lax.axis_index(a) for a in ("z", "y", "core", "tp"))
    inside = (tp // 2) * 4 + core * 2 + tp % 2
    device = y * 8 + inside

    packed_a = do_pack_attention(queries, grad_attn, keys, values)
    packed_a, xs, rates = lax.optimization_barrier((packed_a, xs, rates))
    packed_m = do_pack_mixer(xs, grad_y, bs, cs, dts)
    side = lax.axis_size("tp")
    both = lax.ppermute(
        jnp.stack([rates, skips]),
        ("y", "tp"),
        [(a * side + b, b * side + a) for a in range(side) for b in range(side)],
    )
    mine = lax.dynamic_slice_in_dim(both, inside * HEADS, HEADS, 1)
    my_rates, my_skips = mine[0], mine[1]

    ends = jnp.cumsum(lengths)
    begins = ends - lengths
    base = z * SUPER
    positions = base + jnp.arange(SUPER, dtype=jnp.int32)
    starts = jnp.max(jnp.where(begins[None, :] <= positions[:, None], begins[None, :], 0), axis=1)
    stops = jnp.min(
        jnp.where(ends[None, :] > positions[:, None], ends[None, :], SUPER * 8), axis=1
    )
    block_at = base + jnp.arange(BLOCKS, dtype=jnp.int32) * BLOCK
    last_start = starts[BLOCK - 1 :: BLOCK]
    prior_stop = jnp.min(
        jnp.where(ends[None, :] >= block_at[:, None], ends[None, :], SUPER * 8), axis=1
    )
    entry = jnp.where(block_at > 0, prior_stop - block_at, 0)
    info = jnp.stack(
        [
            last_start - block_at,
            entry,
            (last_start < block_at).astype(jnp.int32),
            jnp.full((BLOCKS,), device, jnp.int32),
        ]
    )
    local_stops = (stops.reshape(BLOCKS, BLOCK) - block_at[:, None]).astype(jnp.int32)

    got_a, packed_m = lax.optimization_barrier((exchange(packed_a), packed_m))
    got_a = got_a.reshape(SUPER, 384)
    own0 = got_a[:, 256:384]
    own1, own2 = shifted(own0, 1), shifted(own0, 2)
    oth0 = swapped(own0)
    packed_m, oth0, my_rates, my_skips = lax.optimization_barrier(
        (packed_m, oth0, my_rates, my_skips)
    )
    got = exchange(packed_m)
    att, keep, send = do_attention(
        jnp.full((1,), core, jnp.int32),
        (starts - (base - 2 * SUPER)).astype(jnp.int32),
        got_a, own0, own1, own2, oth0, swapped(own1), swapped(own2),
    )
    packed_b = do_pack_back(att, keep, swapped(send))
    packed_b, got = lax.optimization_barrier((packed_b, got))
    out_a = exchange(packed_b.reshape(32, ROWS, 640))
    got = got.reshape(SUPER, 896)
    inc, back, factor, send_f, send_b, low, full = do_state(info, my_rates, got)
    got, low = lax.optimization_barrier((got, low))
    f1, f2 = shifted(send_f, 1), shifted(send_f, 2)
    b1, b2 = shifted(send_b, -1), shifted(send_b, -2)
    inner = do_inner(info, my_rates, my_skips, got, local_stops)
    mixed = do_outer(got, inner, low, full, inc, back, factor, f1, f2, b1, b2)
    mixed, out_a = lax.optimization_barrier((mixed, out_a))
    out_m = exchange(mixed.reshape(32, ROWS, 768))
    att, gq, p2, p1, p0 = do_unpack_attention(out_a)
    r1, r2 = shifted(p1, -1), shifted(p2, -2)
    gk, gv = do_add_kv(p0, r1, r2)
    y_out, gx, gb, gc = do_unpack_mixer(out_m)
    return y_out, gx, gb, gc, att, gq, gk, gv


def solution(mesh):
    fine = Mesh(mesh.devices.reshape(-1, 4, 2, 4), ("z", "y", "core", "tp"))
    rows = P(("z", "y", "core", "tp"), None)
    return jax.shard_map(
        per_device,
        mesh=fine,
        in_specs=(rows, rows, rows, rows, P("tp"), P("tp"), rows, rows, rows, P(), rows, rows),
        out_specs=(rows,) * 8,
        check_vma=False,
    )
```

```python
import jax
import jax.numpy as jnp
from jax import lax
from jax.experimental import pallas as pl
from jax.experimental.pallas import tpu as pltpu
from jax.sharding import Mesh, PartitionSpec as P

BF = jnp.bfloat16
F32 = jnp.float32
GROUP = ("y", "core", "tp")
ROWS = 32
SUPER = 1024
BLOCK = 128
BLOCKS = SUPER // BLOCK
HEADS = 4
WIDTH = 64
CH = HEADS * WIDTH
STATE = 128
LANES = 128
SCALE = 128 ** (-0.5)
TQ = 512
TK = 512
UNROLL = 2
ATT = 3.5
NEG = -1e30
NN = (((1,), (0,)), ((), ()))
NT = (((1,), (1,)), ((), ()))
TN = (((0,), (0,)), ((), ()))


def dot(a, b, dims=NN):
    return lax.dot_general(a, b, dims, preferred_element_type=F32)


def params(mib=8):
    return pltpu.CompilerParams(vmem_limit_bytes=mib * 1024 * 1024)


def in_hbm(*arrays):
    return [pltpu.with_memory_space_constraint(a, pltpu.HBM) for a in arrays]


def in_vmem(*arrays):
    return [pltpu.with_memory_space_constraint(a, pltpu.VMEM) for a in arrays]


def cost(micros):
    return pl.CostEstimate(flops=int(micros * 10**9), bytes_accessed=10**6, transcendentals=0)


def smem():
    return pl.BlockSpec(memory_space=pltpu.SMEM)


def vmem():
    return pl.BlockSpec(memory_space=pltpu.VMEM)


def places():
    for core in range(2):
        for tp in range(4):
            yield core, tp // 2, core * 4 + tp, (tp // 2) * 4 + core * 2 + tp % 2


def pack_mixer(x_ref, gy_ref, b_ref, c_ref, dt_ref, out_ref):
    for core, side, at, slot in places():
        out_ref[at, :, 0:256] = x_ref[:, slot * 256 : slot * 256 + 256]
        out_ref[at, :, 256:512] = gy_ref[:, slot * 256 : slot * 256 + 256]
        out_ref[at, :, 512:640] = b_ref[:, side * 128 : side * 128 + 128]
        out_ref[at, :, 640:768] = c_ref[:, side * 128 : side * 128 + 128]
        out_ref[at, :, 768:896] = dt_ref[...]


def pack_attention(q_ref, ga_ref, k_ref, v_ref, out_ref):
    for core, side, at, slot in places():
        out_ref[at, :, 0:128] = q_ref[:, slot * 128 : slot * 128 + 128]
        out_ref[at, :, 128:256] = ga_ref[:, slot * 128 : slot * 128 + 128]
        out_ref[at, :, 256:384] = (k_ref, v_ref)[core][:, side * 128 : side * 128 + 128]


def wide(width, place=0):
    return pl.BlockSpec((ROWS, width), lambda y: (0, y + place))


def do_pack_mixer(xs, gy, bs, cs, dts):
    return pl.pallas_call(
        pack_mixer,
        grid=(4,),
        in_specs=[wide(2048), wide(2048), wide(256), wide(256), pl.BlockSpec((ROWS, 128), lambda y: (0, 0))],
        out_specs=pl.BlockSpec((8, ROWS, 896), lambda y: (y, 0, 0)),
        out_shape=pltpu.HBM((32, ROWS, 896), BF),
        compiler_params=params(),
    )(*in_hbm(xs, gy, bs, cs, dts))


def do_pack_attention(q, ga, keys, values):
    return pl.pallas_call(
        pack_attention,
        grid=(4,),
        in_specs=[wide(1024), wide(1024), wide(256), wide(256)],
        out_specs=pl.BlockSpec((8, ROWS, 384), lambda y: (y, 0, 0)),
        out_shape=pltpu.HBM((32, ROWS, 384), BF),
        compiler_params=params(),
    )(*in_hbm(q, ga, keys, values))


def unpack_mixer(in_ref, y_ref, gx_ref, gb_ref, gc_ref):
    gb = [jnp.zeros((ROWS, 128), F32)] * 2
    gc = [jnp.zeros((ROWS, 128), F32)] * 2
    for core, side, at, slot in places():
        y_ref[:, slot * 256 : slot * 256 + 256] = in_ref[at, :, 0:256]
        gx_ref[:, slot * 256 : slot * 256 + 256] = in_ref[at, :, 256:512]
        gb[side] = gb[side] + in_ref[at, :, 512:640].astype(F32)
        gc[side] = gc[side] + in_ref[at, :, 640:768].astype(F32)
    gb_ref[...] = jnp.concatenate(gb, axis=1).astype(BF)
    gc_ref[...] = jnp.concatenate(gc, axis=1).astype(BF)


def do_unpack_mixer(got):
    return pl.pallas_call(
        unpack_mixer,
        grid=(4,),
        in_specs=[pl.BlockSpec((8, ROWS, 768), lambda y: (y, 0, 0))],
        out_specs=[wide(2048), wide(2048), wide(256), wide(256)],
        out_shape=[
            jax.ShapeDtypeStruct((ROWS, 8192), BF),
            jax.ShapeDtypeStruct((ROWS, 8192), BF),
            jax.ShapeDtypeStruct((ROWS, 1024), BF),
            jax.ShapeDtypeStruct((ROWS, 1024), BF),
        ],
        compiler_params=params(),
    )(got)


def unpack_attention(in_ref, att_ref, gq_ref, two_ref, one_ref, own_ref):
    refs = (two_ref, one_ref, own_ref)
    totals = {}
    for core, side, at, slot in places():
        att_ref[:, slot * 128 : slot * 128 + 128] = in_ref[at, :, 0:128]
        gq_ref[:, slot * 128 : slot * 128 + 128] = in_ref[at, :, 128:256]
        for n in range(3):
            part = in_ref[at, :, 256 + n * 128 : 384 + n * 128].astype(F32)
            where = (n, core, side)
            totals[where] = totals[where] + part if where in totals else part
    for (n, core, side), total in totals.items():
        col = core * 256 + side * 128
        refs[n][:, col : col + 128] = total.astype(refs[n].dtype)


def do_unpack_attention(got):
    return pl.pallas_call(
        unpack_attention,
        grid=(4,),
        in_specs=[pl.BlockSpec((8, ROWS, 640), lambda y: (y, 0, 0))],
        out_specs=[wide(1024), wide(1024), wide(512), wide(512), wide(512)],
        out_shape=[
            jax.ShapeDtypeStruct((ROWS, 4096), BF),
            jax.ShapeDtypeStruct((ROWS, 4096), BF),
            jax.ShapeDtypeStruct((ROWS, 2048), BF),
            jax.ShapeDtypeStruct((ROWS, 2048), BF),
            jax.ShapeDtypeStruct((ROWS, 2048), F32),
        ],
        compiler_params=params(),
    )(got)


def add_kv(own_ref, one_ref, two_ref, gk_ref, gv_ref):
    for y in range(4):
        at = slice(y * 512, y * 512 + 512)
        total = (own_ref[:, at] + one_ref[:, at].astype(F32) + two_ref[:, at].astype(F32)).astype(BF)
        gk_ref[:, y * 256 : y * 256 + 256] = total[:, 0:256]
        gv_ref[:, y * 256 : y * 256 + 256] = total[:, 256:512]


def do_add_kv(own, one, two):
    return pl.pallas_call(
        add_kv,
        in_specs=[vmem()] * 3,
        out_specs=[vmem()] * 2,
        out_shape=[jax.ShapeDtypeStruct((ROWS, 1024), BF)] * 2,
        compiler_params=params(),
    )(own, one, two)


def pack_back(att_ref, keep_ref, come_ref, out_ref):
    out_ref[:, 0:256] = att_ref[...]
    for n in range(3):
        rows = slice(n * SUPER, n * SUPER + SUPER)
        total = keep_ref[rows, :].astype(F32) + come_ref[rows, :].astype(F32)
        out_ref[:, 256 + n * 128 : 384 + n * 128] = total.astype(BF)


def do_pack_back(att, keep, come):
    return pl.pallas_call(
        pack_back,
        in_specs=[vmem()] * 3,
        out_specs=vmem(),
        out_shape=pltpu.HBM((SUPER, 640), BF),
        compiler_params=params(),
    )(*in_hbm(att, keep), come)


def lane_row(values, width):
    lane = lax.broadcasted_iota(jnp.int32, (1, width * HEADS), 1)
    row = jnp.full((1, width * HEADS), values[0], F32)
    for h in range(1, HEADS):
        row = jnp.where(lane >= h * width, values[h], row)
    return row


def lower(n):
    return (
        lax.broadcasted_iota(jnp.int32, (n, n), 1) <= lax.broadcasted_iota(jnp.int32, (n, n), 0)
    ).astype(F32).astype(BF)


def upper(n):
    return (
        lax.broadcasted_iota(jnp.int32, (n, n), 0) <= lax.broadcasted_iota(jnp.int32, (n, n), 1)
    ).astype(F32).astype(BF)


def pick(first, width):
    head = lax.broadcasted_iota(jnp.int32, (128, width * HEADS), 0) - first
    lane = lax.broadcasted_iota(jnp.int32, (128, width * HEADS), 1) // width
    return (head == lane).astype(F32).astype(BF)


def channel_decay(dts, chooser, tri, rate_row, tail, entry):
    steps = dot(dts, chooser)
    cumul = dot(tri, steps.astype(BF)) * (-rate_row)
    end = cumul[BLOCK - 1 : BLOCK, :]
    row = lax.broadcasted_iota(jnp.int32, (BLOCK, CH), 0)
    weight = jnp.where(row >= tail, jnp.exp(end - cumul), 0.0)
    enter = jnp.where(row < entry, jnp.exp(cumul), 0.0)
    return steps, steps * weight, enter, end


def state_kernel(
    info, rates, in_ref, inc_ref, out_ref, factor_ref, sf_ref, sb_ref, low_ref, full_ref
):
    first = info[3, 0] * HEADS
    tri = lower(BLOCK)
    chooser = pick(first, WIDTH)
    rate_row = lane_row([rates[h] for h in range(HEADS)], WIDTH)
    state = jnp.zeros((STATE, CH), F32)
    prefix = jnp.ones((1, CH), F32)
    carries = []
    pulled = []
    for j in range(BLOCKS):
        rows = slice(j * BLOCK, j * BLOCK + BLOCK)
        tail, entry, alive = info[0, j], info[1, j], info[2, j]
        _, weighted, enter, end = channel_decay(
            in_ref[rows, 768:896], chooser, tri, rate_row, tail, entry
        )
        scaled = (in_ref[rows, 0:256].astype(F32) * weighted).astype(BF)
        dcar = (in_ref[rows, 256:512].astype(F32) * enter).astype(BF)
        low_ref[rows, 0:256] = scaled
        low_ref[rows, 256:512] = dcar
        full_ref[rows, 0:256] = weighted
        full_ref[rows, 256:512] = enter
        carry = jnp.where(alive > 0, jnp.exp(end), 0.0)
        inc_ref[j] = state
        factor_ref[j : j + 1, :] = prefix
        state = carry * state + dot(in_ref[rows, 512:640], scaled, TN)
        prefix = prefix * carry
        carries.append(carry)
        pulled.append(dot(in_ref[rows, 640:768], dcar, TN))
    high = prefix.astype(BF)
    low = (prefix - high.astype(F32)).astype(BF)
    place = lax.broadcasted_iota(jnp.int32, (16, CH), 0)
    extra = jnp.where(place == 0, high.astype(F32), jnp.where(place == 1, low.astype(F32), 0.0)).astype(BF)
    sf_ref[0:128, :] = state.astype(BF)
    sf_ref[128:144, :] = extra
    back = jnp.zeros((STATE, CH), F32)
    suffix = jnp.ones((1, CH), F32)
    for j in range(BLOCKS - 1, -1, -1):
        out_ref[j] = back
        factor_ref[8 + j : 9 + j, :] = suffix
        back = pulled[j] + carries[j] * back
        suffix = suffix * carries[j]
    sb_ref[0:128, :] = back.astype(BF)
    sb_ref[128:144, :] = extra


def do_state(info, rates, got):
    return pl.pallas_call(
        state_kernel,
        in_specs=[smem(), smem(), vmem()],
        out_specs=[vmem()] * 7,
        out_shape=[
            pltpu.VMEM((BLOCKS, STATE, CH), F32),
            pltpu.VMEM((BLOCKS, STATE, CH), F32),
            pltpu.VMEM((16, CH), F32),
            jax.ShapeDtypeStruct((144, CH), BF),
            jax.ShapeDtypeStruct((144, CH), BF),
            pltpu.VMEM((SUPER, 512), BF),
            pltpu.VMEM((SUPER, 512), F32),
        ],
        compiler_params=params(12),
        cost_estimate=cost(3),
    )(info, rates, *in_vmem(got))


def joined(one_ref, two_ref):
    decay = one_ref[128:129, :].astype(F32) + one_ref[129:130, :].astype(F32)
    return one_ref[0:128, :].astype(F32) + decay * two_ref[0:128, :].astype(F32)


def inner_kernel(info, rates, skips, in_ref, ends_ref, out_ref):
    first = info[3, 0] * HEADS
    tri = lower(BLOCK)
    triu = upper(BLOCK)
    chooser = pick(first, WIDTH)
    column_chooser = pick(first, LANES)
    head_row = lax.broadcasted_iota(jnp.int32, (8, 128), 0)
    head_at = lax.broadcasted_iota(jnp.int32, (8, 128), 1) - first
    row_chooser = ((head_row == head_at) & (head_row < HEADS)).astype(F32).astype(BF)
    skip_row = lane_row([skips[h] for h in range(HEADS)], WIDTH)
    t_at = lax.broadcasted_iota(jnp.int32, (BLOCK, BLOCK), 0)
    s_at = lax.broadcasted_iota(jnp.int32, (BLOCK, BLOCK), 1)
    lane = lax.broadcasted_iota(jnp.int32, (BLOCK, CH), 1)
    owns = [(lane >= h * WIDTH) & (lane < (h + 1) * WIDTH) for h in range(HEADS)]

    def one(j, _):
        rows = pl.ds(pl.multiple_of(j * BLOCK, BLOCK), BLOCK)
        dts = in_ref[rows, 768:896]
        steps = dot(dts, chooser)
        x = in_ref[rows, 0:256].astype(F32)
        gy_low = in_ref[rows, 256:512]
        b = in_ref[rows, 512:640]
        c = in_ref[rows, 640:768]
        columns = dot(tri, dot(dts, column_chooser).astype(BF))
        lines = dot(dot(row_chooser, dts, NT).astype(BF), triu)
        ends = ends_ref[pl.ds(j, 1), :]
        mask = (s_at <= t_at) & (t_at < ends)
        scores = dot(c, b, NT)
        driven = x * steps
        decays = []
        mixes = []
        drives = []
        for h in range(HEADS):
            gap = (columns[:, h * 128 : h * 128 + 128] - lines[h : h + 1, :]) * (-rates[h])
            decay = jnp.exp(jnp.where(mask, gap, NEG))
            decays.append(decay)
            mixes.append((decay * scores).astype(BF))
            drives.append(jnp.where(owns[h], driven, 0.0).astype(BF))
        mix = jnp.concatenate(mixes, axis=1)
        drive = jnp.concatenate(drives, axis=0)
        out_ref[rows, 0:256] = dot(mix, drive) + skip_row * x
        grad_mix = dot(gy_low, drive, NT)
        grad_scores = decays[0] * grad_mix[:, 0:128]
        for h in range(1, HEADS):
            grad_scores = grad_scores + decays[h] * grad_mix[:, h * 128 : h * 128 + 128]
        grad_low = grad_scores.astype(BF)
        back = dot(mix, gy_low, TN)
        grad_drive = jnp.where(owns[0], back[0:128], 0.0)
        for h in range(1, HEADS):
            grad_drive = jnp.where(owns[h], back[h * 128 : h * 128 + 128], grad_drive)
        out_ref[rows, 256:512] = grad_drive * steps + skip_row * gy_low.astype(F32)
        out_ref[rows, 512:640] = dot(grad_low, c, TN)
        out_ref[rows, 640:768] = dot(grad_low, b)
        return 0

    lax.fori_loop(0, BLOCKS, one, 0, unroll=UNROLL)


def do_inner(info, rates, skips, got, ends):
    return pl.pallas_call(
        inner_kernel,
        in_specs=[smem()] * 3 + [vmem()] * 2,
        out_specs=vmem(),
        out_shape=pltpu.VMEM((SUPER, 768), F32),
        compiler_params=params(12),
        cost_estimate=cost(8),
    )(info, rates, skips, *in_vmem(got), ends)


def outer_kernel(
    in_ref, part_ref, low_ref, full_ref, inc_ref, back_ref, factor_ref, f1, f2, b1, b2, out_ref
):
    entering = joined(f1, f2)
    leaving = joined(b1, b2)
    for j in range(BLOCKS):
        rows = slice(j * BLOCK, j * BLOCK + BLOCK)
        b = in_ref[rows, 512:640]
        c = in_ref[rows, 640:768]
        state = (inc_ref[j] + factor_ref[j : j + 1, :] * entering).astype(BF)
        pull = (back_ref[j] + factor_ref[8 + j : 9 + j, :] * leaving).astype(BF)
        y = part_ref[rows, 0:256] + dot(c, state) * full_ref[rows, 256:512]
        gx = part_ref[rows, 256:512] + dot(b, pull) * full_ref[rows, 0:256]
        gb = part_ref[rows, 512:640] + dot(low_ref[rows, 0:256], pull, NT)
        gc = part_ref[rows, 640:768] + dot(low_ref[rows, 256:512], state, NT)
        out_ref[rows, 0:256] = y.astype(BF)
        out_ref[rows, 256:512] = gx.astype(BF)
        out_ref[rows, 512:640] = gb.astype(BF)
        out_ref[rows, 640:768] = gc.astype(BF)


def do_outer(*operands):
    return pl.pallas_call(
        outer_kernel,
        in_specs=[vmem()] * 11,
        out_specs=vmem(),
        out_shape=pltpu.HBM((SUPER, 768), BF),
        compiler_params=params(16),
        cost_estimate=cost(2),
    )(*in_vmem(*operands))


def attention_kernel(
    core, starts, in_ref, own0, own1, own2, oth0, oth1, oth2, start_ref, out_ref, keep_ref, send_ref,
    k_ref, v_ref, kt_ref, vt_ref, near_ref, far_ref, peak_ref, gk_ref, gv_ref, sems
):
    count = SUPER // TQ
    lowest = starts[0] - TK + 1
    places_of = [slice(n * SUPER, n * SUPER + SUPER) for n in range(3)]
    owns = (own2, own1, own0)
    others = (oth2, oth1, oth0)

    def moves(n, first):
        mine, theirs = (owns[n], others[n]) if first else (others[n], owns[n])
        return (
            pltpu.make_async_copy(mine, k_ref.at[places_of[n], :], sems.at[2 * n]),
            pltpu.make_async_copy(theirs, v_ref.at[places_of[n], :], sems.at[2 * n + 1]),
        )

    def on_core(n, first, act):
        @pl.when((lowest < (n + 1) * SUPER) & ((core[0] == 0) == first))
        def _():
            for move in moves(n, first):
                act(move)

    for n in (2, 1, 0):
        on_core(n, True, lambda move: move.start())
        on_core(n, False, lambda move: move.start())
    gk_ref[...] = jnp.zeros_like(gk_ref)
    gv_ref[...] = jnp.zeros_like(gv_ref)
    for n in (2, 1, 0):
        on_core(n, True, lambda move: move.wait())
        on_core(n, False, lambda move: move.wait())

        @pl.when(lowest < (n + 1) * SUPER)
        def _():
            kt_ref[:, places_of[n]] = k_ref[places_of[n], :].T
            vt_ref[:, places_of[n]] = v_ref[places_of[n], :].T

    def tile_sum(p):
        return jnp.sum(p.reshape(p.shape[0] // 8, 8, TQ), axis=0)

    at = lax.broadcasted_iota(jnp.int32, (TQ, TQ), 0)
    here = lax.broadcasted_iota(jnp.int32, (TQ, TQ), 1)
    far_at = lax.broadcasted_iota(jnp.int32, (TK, TQ), 0)
    q_rows = [slice(i * TQ, i * TQ + TQ) for i in range(count)]
    diag = [2 * SUPER + i * TQ for i in range(count)]
    near = [slice(diag[i], diag[i] + TQ) for i in range(count)]
    begins = [start_ref[i : i + 1, :] for i in range(count)]
    many = [(jnp.maximum(diag[i] - starts[i * TQ], 0) + TK - 1) // TK for i in range(count)]

    carries = []
    for i in range(count):
        q = in_ref[q_rows[i], 0:128]
        s = dot(k_ref[near[i], :], q, NT)
        s = jnp.where((at + diag[i] >= begins[i]) & (at <= here), s, NEG)
        peak = jnp.max(s, axis=0, keepdims=True)
        p = jnp.exp((s - peak) * SCALE)
        p_low = p.astype(BF)
        near_ref[i] = p_low
        peak_ref[i, 4:5, :] = peak
        carries.append((peak, tile_sum(p), dot(vt_ref[:, near[i]], p_low)))

    def forward(i, t, carry):
        peak, total, att = carry
        base = diag[i] - TK * (t + 1)
        rows = pl.ds(pl.multiple_of(base, TQ), TK)
        s = dot(k_ref[rows, :], in_ref[q_rows[i], 0:128], NT)
        s = jnp.where(far_at >= begins[i] - base, s, NEG)
        top = jnp.maximum(peak, jnp.max(s, axis=0, keepdims=True))
        alpha = jnp.exp((peak - top) * SCALE)
        p = jnp.exp((s - top) * SCALE)
        p_low = p.astype(BF)
        far_ref[i, t] = p_low
        peak_ref[i, pl.ds(t, 1), :] = top
        att = att * alpha + dot(vt_ref[:, rows], p_low)
        return top, total * alpha + tile_sum(p), att

    def paired(step, carries):
        shared = many[0]
        for other in many[1:]:
            shared = jnp.minimum(shared, other)
        carries = lax.fori_loop(
            0, shared, lambda t, c: tuple(step(i, t, c[i]) for i in range(count)), tuple(carries)
        )
        return [
            lax.fori_loop(shared, many[i], lambda t, c, i=i: step(i, t, c), carries[i])
            for i in range(count)
        ]

    carries = paired(forward, carries)

    def grads(i, t, rows, p_low, peak, inverse, delta, ga_turned):
        factor = jnp.exp((peak_ref[i, pl.ds(t, 1), :] - peak) * SCALE) * inverse
        ga = (ga_turned * factor).astype(BF)
        ds = (p_low.astype(F32) * (dot(v_ref[rows, :], ga) - delta * factor)).astype(BF)
        gk_ref[rows, :] += dot(ds, in_ref[q_rows[i], 0:128])
        gv_ref[rows, :] += dot(p_low, ga, NT)
        return dot(kt_ref[:, rows], ds)

    rest = []
    for i in range(count):
        peak, total, att = carries[i]
        ga_turned = in_ref[q_rows[i], 128:256].T.astype(F32)
        inverse = 1.0 / jnp.sum(total, axis=0, keepdims=True)
        att = (att * inverse).astype(BF)
        out_ref[q_rows[i], 0:128] = att.T
        delta = jnp.sum(ga_turned * att.astype(F32), axis=0, keepdims=True)
        state = (peak, inverse, delta, ga_turned)
        rest.append((state, grads(i, 4, near[i], near_ref[i], *state)))

    def backward(i, t, gq):
        rows = pl.ds(pl.multiple_of(diag[i] - TK * (t + 1), TQ), TK)
        return gq + grads(i, t, rows, far_ref[i, t], *rest[i][0])

    for i, gq in enumerate(paired(backward, [gq for _, gq in rest])):
        out_ref[q_rows[i], 128:256] = (gq * SCALE).astype(BF).T

    def store(k_out, v_out):
        k_out[...] = (gk_ref[...] * SCALE).astype(BF)
        v_out[...] = gv_ref[...].astype(BF)

    @pl.when(core[0] == 0)
    def _():
        store(keep_ref, send_ref)

    @pl.when(core[0] != 0)
    def _():
        store(send_ref, keep_ref)


def do_attention(core, starts, *moved):
    span = 3 * SUPER
    count = SUPER // TQ
    return pl.pallas_call(
        attention_kernel,
        in_specs=[smem()] * 2 + [vmem()] + [pl.BlockSpec(memory_space=pl.ANY)] * 6 + [vmem()],
        out_specs=[vmem()] * 3,
        out_shape=[
            pltpu.HBM((SUPER, 256), BF),
            pltpu.HBM((3 * SUPER, 128), BF),
            pltpu.HBM((3 * SUPER, 128), BF),
        ],
        scratch_shapes=[
            pltpu.VMEM((span, 128), BF),
            pltpu.VMEM((span, 128), BF),
            pltpu.VMEM((128, span), BF),
            pltpu.VMEM((128, span), BF),
            pltpu.VMEM((count, TQ, TQ), BF),
            pltpu.VMEM((count, 4, TK, TQ), BF),
            pltpu.VMEM((count, 8, TQ), F32),
            pltpu.VMEM((span, 128), F32),
            pltpu.VMEM((span, 128), F32),
            pltpu.SemaphoreType.DMA((6,)),
        ],
        compiler_params=params(28),
        cost_estimate=cost(ATT),
    )(core, starts, *moved, starts.reshape(SUPER // TQ, TQ))


def shifted(block, distance):
    count = lax.axis_size("z")
    route = [(i, i + distance) for i in range(count) if 0 <= i + distance < count]
    return lax.ppermute(block, "z", route)


def exchange(block):
    return lax.all_to_all(block, GROUP, split_axis=0, concat_axis=0, tiled=True)


def swapped(block):
    return lax.ppermute(block, "core", [(0, 1), (1, 0)])


def per_device(xs, dts, bs, cs, rates, skips, queries, keys, values, lengths, grad_y, grad_attn):
    z, y, core, tp = (lax.axis_index(a) for a in ("z", "y", "core", "tp"))
    inside = (tp // 2) * 4 + core * 2 + tp % 2
    device = y * 8 + inside

    packed_a = do_pack_attention(queries, grad_attn, keys, values)
    packed_a, xs, rates = lax.optimization_barrier((packed_a, xs, rates))
    packed_m = do_pack_mixer(xs, grad_y, bs, cs, dts)
    side = lax.axis_size("tp")
    both = lax.ppermute(
        jnp.stack([rates, skips]),
        ("y", "tp"),
        [(a * side + b, b * side + a) for a in range(side) for b in range(side)],
    )
    mine = lax.dynamic_slice_in_dim(both, inside * HEADS, HEADS, 1)
    my_rates, my_skips = mine[0], mine[1]

    ends = jnp.cumsum(lengths)
    begins = ends - lengths
    base = z * SUPER
    positions = base + jnp.arange(SUPER, dtype=jnp.int32)
    starts = jnp.max(jnp.where(begins[None, :] <= positions[:, None], begins[None, :], 0), axis=1)
    stops = jnp.min(
        jnp.where(ends[None, :] > positions[:, None], ends[None, :], SUPER * 8), axis=1
    )
    block_at = base + jnp.arange(BLOCKS, dtype=jnp.int32) * BLOCK
    last_start = starts[BLOCK - 1 :: BLOCK]
    prior_stop = jnp.min(
        jnp.where(ends[None, :] >= block_at[:, None], ends[None, :], SUPER * 8), axis=1
    )
    entry = jnp.where(block_at > 0, prior_stop - block_at, 0)
    info = jnp.stack(
        [
            last_start - block_at,
            entry,
            (last_start < block_at).astype(jnp.int32),
            jnp.full((BLOCKS,), device, jnp.int32),
        ]
    )
    local_stops = (stops.reshape(BLOCKS, BLOCK) - block_at[:, None]).astype(jnp.int32)

    got_a, packed_m = lax.optimization_barrier((exchange(packed_a), packed_m))
    got_a = got_a.reshape(SUPER, 384)
    own0 = got_a[:, 256:384]
    own1 = shifted(own0, 1)
    own2 = shifted(own1, 1)
    oth0 = swapped(own0)
    packed_m, oth0, my_rates, my_skips = lax.optimization_barrier(
        (packed_m, oth0, my_rates, my_skips)
    )
    got = exchange(packed_m)
    att, keep, send = do_attention(
        jnp.full((1,), core, jnp.int32),
        (starts - (base - 2 * SUPER)).astype(jnp.int32),
        got_a, own0, own1, own2, oth0, swapped(own1), swapped(own2),
    )
    packed_b = do_pack_back(att, keep, swapped(send))
    packed_b, got = lax.optimization_barrier((packed_b, got))
    out_a = exchange(packed_b.reshape(32, ROWS, 640))
    got = got.reshape(SUPER, 896)
    inc, back, factor, send_f, send_b, low, full = do_state(info, my_rates, got)
    got, low = lax.optimization_barrier((got, low))
    f1, f2 = shifted(send_f, 1), shifted(send_f, 2)
    b1, b2 = shifted(send_b, -1), shifted(send_b, -2)
    inner = do_inner(info, my_rates, my_skips, got, local_stops)
    mixed = do_outer(got, inner, low, full, inc, back, factor, f1, f2, b1, b2)
    mixed, out_a = lax.optimization_barrier((mixed, out_a))
    out_m = exchange(mixed.reshape(32, ROWS, 768))
    att, gq, p2, p1, p0 = do_unpack_attention(out_a)
    r1, r2 = shifted(p1, -1), shifted(p2, -2)
    gk, gv = do_add_kv(p0, r1, r2)
    y_out, gx, gb, gc = do_unpack_mixer(out_m)
    return y_out, gx, gb, gc, att, gq, gk, gv


def solution(mesh):
    fine = Mesh(mesh.devices.reshape(-1, 4, 2, 4), ("z", "y", "core", "tp"))
    rows = P(("z", "y", "core", "tp"), None)
    return jax.shard_map(
        per_device,
        mesh=fine,
        in_specs=(rows, rows, rows, rows, P("tp"), P("tp"), rows, rows, rows, P(), rows, rows),
        out_specs=(rows,) * 8,
        check_vma=False,
    )
```

```python
import jax
import jax.numpy as jnp
from jax import lax
from jax.experimental import pallas as pl
from jax.experimental.pallas import tpu as pltpu
from jax.sharding import Mesh, PartitionSpec as P

BF = jnp.bfloat16
F32 = jnp.float32
GROUP = ("y", "core", "tp")
ROWS = 32
SUPER = 1024
BLOCK = 128
BLOCKS = SUPER // BLOCK
HEADS = 4
WIDTH = 64
CH = HEADS * WIDTH
STATE = 128
LANES = 128
SCALE = 128 ** (-0.5)
TQ = 512
TK = 512
HALF = 256
UNROLL = 4
ATT = 3.5
NEG = -1e30
NN = (((1,), (0,)), ((), ()))
NT = (((1,), (1,)), ((), ()))
TN = (((0,), (0,)), ((), ()))


def dot(a, b, dims=NN):
    return lax.dot_general(a, b, dims, preferred_element_type=F32)


def params(mib=8):
    return pltpu.CompilerParams(vmem_limit_bytes=mib * 1024 * 1024)


def in_hbm(*arrays):
    return [pltpu.with_memory_space_constraint(a, pltpu.HBM) for a in arrays]


def in_vmem(*arrays):
    return [pltpu.with_memory_space_constraint(a, pltpu.VMEM) for a in arrays]


def cost(micros):
    return pl.CostEstimate(flops=int(micros * 10**9), bytes_accessed=10**6, transcendentals=0)


def smem():
    return pl.BlockSpec(memory_space=pltpu.SMEM)


def vmem():
    return pl.BlockSpec(memory_space=pltpu.VMEM)


def places():
    for core in range(2):
        for tp in range(4):
            yield core, tp // 2, core * 4 + tp, (tp // 2) * 4 + core * 2 + tp % 2


def pack_mixer(x_ref, gy_ref, b_ref, c_ref, dt_ref, out_ref):
    for core, side, at, slot in places():
        out_ref[at, :, 0:256] = x_ref[:, slot * 256 : slot * 256 + 256]
        out_ref[at, :, 256:512] = gy_ref[:, slot * 256 : slot * 256 + 256]
        out_ref[at, :, 512:640] = b_ref[:, side * 128 : side * 128 + 128]
        out_ref[at, :, 640:768] = c_ref[:, side * 128 : side * 128 + 128]
        out_ref[at, :, 768:896] = dt_ref[...]


def pack_attention(q_ref, ga_ref, k_ref, v_ref, out_ref):
    for core, side, at, slot in places():
        out_ref[at, :, 0:128] = q_ref[:, slot * 128 : slot * 128 + 128]
        out_ref[at, :, 128:256] = ga_ref[:, slot * 128 : slot * 128 + 128]
        out_ref[at, :, 256:384] = (k_ref, v_ref)[core][:, side * 128 : side * 128 + 128]


def wide(width, place=0):
    return pl.BlockSpec((ROWS, width), lambda y: (0, y + place))


def do_pack_mixer(xs, gy, bs, cs, dts):
    return pl.pallas_call(
        pack_mixer,
        grid=(4,),
        in_specs=[wide(2048), wide(2048), wide(256), wide(256), pl.BlockSpec((ROWS, 128), lambda y: (0, 0))],
        out_specs=pl.BlockSpec((8, ROWS, 896), lambda y: (y, 0, 0)),
        out_shape=pltpu.HBM((32, ROWS, 896), BF),
        compiler_params=params(),
    )(*in_hbm(xs, gy, bs, cs, dts))


def do_pack_attention(q, ga, keys, values):
    return pl.pallas_call(
        pack_attention,
        grid=(4,),
        in_specs=[wide(1024), wide(1024), wide(256), wide(256)],
        out_specs=pl.BlockSpec((8, ROWS, 384), lambda y: (y, 0, 0)),
        out_shape=pltpu.HBM((32, ROWS, 384), BF),
        compiler_params=params(),
    )(*in_hbm(q, ga, keys, values))


def unpack_mixer(in_ref, y_ref, gx_ref, gb_ref, gc_ref):
    gb = [jnp.zeros((ROWS, 128), F32)] * 2
    gc = [jnp.zeros((ROWS, 128), F32)] * 2
    for core, side, at, slot in places():
        y_ref[:, slot * 256 : slot * 256 + 256] = in_ref[at, :, 0:256]
        gx_ref[:, slot * 256 : slot * 256 + 256] = in_ref[at, :, 256:512]
        gb[side] = gb[side] + in_ref[at, :, 512:640].astype(F32)
        gc[side] = gc[side] + in_ref[at, :, 640:768].astype(F32)
    gb_ref[...] = jnp.concatenate(gb, axis=1).astype(BF)
    gc_ref[...] = jnp.concatenate(gc, axis=1).astype(BF)


def do_unpack_mixer(got):
    return pl.pallas_call(
        unpack_mixer,
        grid=(4,),
        in_specs=[pl.BlockSpec((8, ROWS, 768), lambda y: (y, 0, 0))],
        out_specs=[wide(2048), wide(2048), wide(256), wide(256)],
        out_shape=[
            jax.ShapeDtypeStruct((ROWS, 8192), BF),
            jax.ShapeDtypeStruct((ROWS, 8192), BF),
            jax.ShapeDtypeStruct((ROWS, 1024), BF),
            jax.ShapeDtypeStruct((ROWS, 1024), BF),
        ],
        compiler_params=params(),
    )(got)


def unpack_attention(in_ref, att_ref, gq_ref, two_ref, one_ref, own_ref):
    refs = (two_ref, one_ref, own_ref)
    totals = {}
    for core, side, at, slot in places():
        att_ref[:, slot * 128 : slot * 128 + 128] = in_ref[at, :, 0:128]
        gq_ref[:, slot * 128 : slot * 128 + 128] = in_ref[at, :, 128:256]
        for n in range(3):
            part = in_ref[at, :, 256 + n * 128 : 384 + n * 128].astype(F32)
            where = (n, core, side)
            totals[where] = totals[where] + part if where in totals else part
    for (n, core, side), total in totals.items():
        col = core * 256 + side * 128
        refs[n][:, col : col + 128] = total.astype(refs[n].dtype)


def do_unpack_attention(got):
    return pl.pallas_call(
        unpack_attention,
        grid=(4,),
        in_specs=[pl.BlockSpec((8, ROWS, 640), lambda y: (y, 0, 0))],
        out_specs=[wide(1024), wide(1024), wide(512), wide(512), wide(512)],
        out_shape=[
            jax.ShapeDtypeStruct((ROWS, 4096), BF),
            jax.ShapeDtypeStruct((ROWS, 4096), BF),
            jax.ShapeDtypeStruct((ROWS, 2048), BF),
            jax.ShapeDtypeStruct((ROWS, 2048), BF),
            jax.ShapeDtypeStruct((ROWS, 2048), F32),
        ],
        compiler_params=params(),
    )(got)


def add_kv(own_ref, one_ref, two_ref, gk_ref, gv_ref):
    for y in range(4):
        at = slice(y * 512, y * 512 + 512)
        total = (own_ref[:, at] + one_ref[:, at].astype(F32) + two_ref[:, at].astype(F32)).astype(BF)
        gk_ref[:, y * 256 : y * 256 + 256] = total[:, 0:256]
        gv_ref[:, y * 256 : y * 256 + 256] = total[:, 256:512]


def do_add_kv(own, one, two):
    return pl.pallas_call(
        add_kv,
        in_specs=[vmem()] * 3,
        out_specs=[vmem()] * 2,
        out_shape=[jax.ShapeDtypeStruct((ROWS, 1024), BF)] * 2,
        compiler_params=params(),
    )(own, one, two)


def pack_back(att_ref, keep_ref, come_ref, out_ref):
    out_ref[:, 0:256] = att_ref[...]
    for n in range(3):
        rows = slice(n * SUPER, n * SUPER + SUPER)
        total = keep_ref[rows, :].astype(F32) + come_ref[rows, :].astype(F32)
        out_ref[:, 256 + n * 128 : 384 + n * 128] = total.astype(BF)


def do_pack_back(att, keep, come):
    return pl.pallas_call(
        pack_back,
        in_specs=[vmem()] * 3,
        out_specs=vmem(),
        out_shape=pltpu.HBM((SUPER, 640), BF),
        compiler_params=params(),
    )(*in_hbm(att, keep), come)


def lane_row(values, width):
    lane = lax.broadcasted_iota(jnp.int32, (1, width * HEADS), 1)
    row = jnp.full((1, width * HEADS), values[0], F32)
    for h in range(1, HEADS):
        row = jnp.where(lane >= h * width, values[h], row)
    return row


def lower(n):
    return (
        lax.broadcasted_iota(jnp.int32, (n, n), 1) <= lax.broadcasted_iota(jnp.int32, (n, n), 0)
    ).astype(F32).astype(BF)


def upper(n):
    return (
        lax.broadcasted_iota(jnp.int32, (n, n), 0) <= lax.broadcasted_iota(jnp.int32, (n, n), 1)
    ).astype(F32).astype(BF)


def pick(first, width):
    head = lax.broadcasted_iota(jnp.int32, (128, width * HEADS), 0) - first
    lane = lax.broadcasted_iota(jnp.int32, (128, width * HEADS), 1) // width
    return (head == lane).astype(F32).astype(BF)


def channel_decay(dts, chooser, tri, rate_row, tail, entry):
    steps = dot(dts, chooser)
    cumul = dot(tri, steps.astype(BF)) * (-rate_row)
    end = cumul[BLOCK - 1 : BLOCK, :]
    row = lax.broadcasted_iota(jnp.int32, (BLOCK, CH), 0)
    weight = jnp.where(row >= tail, jnp.exp(end - cumul), 0.0)
    enter = jnp.where(row < entry, jnp.exp(cumul), 0.0)
    return steps, steps * weight, enter, end


def state_kernel(
    info, rates, in_ref, inc_ref, out_ref, factor_ref, sf_ref, sb_ref, low_ref, full_ref
):
    first = info[3, 0] * HEADS
    tri = lower(BLOCK)
    chooser = pick(first, WIDTH)
    rate_row = lane_row([rates[h] for h in range(HEADS)], WIDTH)
    state = jnp.zeros((STATE, CH), F32)
    prefix = jnp.ones((1, CH), F32)
    carries = []
    pulled = []
    for j in range(BLOCKS):
        rows = slice(j * BLOCK, j * BLOCK + BLOCK)
        tail, entry, alive = info[0, j], info[1, j], info[2, j]
        _, weighted, enter, end = channel_decay(
            in_ref[rows, 768:896], chooser, tri, rate_row, tail, entry
        )
        scaled = (in_ref[rows, 0:256].astype(F32) * weighted).astype(BF)
        dcar = (in_ref[rows, 256:512].astype(F32) * enter).astype(BF)
        low_ref[rows, 0:256] = scaled
        low_ref[rows, 256:512] = dcar
        full_ref[rows, 0:256] = weighted
        full_ref[rows, 256:512] = enter
        carry = jnp.where(alive > 0, jnp.exp(end), 0.0)
        inc_ref[j] = state
        factor_ref[j : j + 1, :] = prefix
        state = carry * state + dot(in_ref[rows, 512:640], scaled, TN)
        prefix = prefix * carry
        carries.append(carry)
        pulled.append(dot(in_ref[rows, 640:768], dcar, TN))
    high = prefix.astype(BF)
    low = (prefix - high.astype(F32)).astype(BF)
    place = lax.broadcasted_iota(jnp.int32, (16, CH), 0)
    extra = jnp.where(place == 0, high.astype(F32), jnp.where(place == 1, low.astype(F32), 0.0)).astype(BF)
    sf_ref[0:128, :] = state.astype(BF)
    sf_ref[128:144, :] = extra
    back = jnp.zeros((STATE, CH), F32)
    suffix = jnp.ones((1, CH), F32)
    for j in range(BLOCKS - 1, -1, -1):
        out_ref[j] = back
        factor_ref[8 + j : 9 + j, :] = suffix
        back = pulled[j] + carries[j] * back
        suffix = suffix * carries[j]
    sb_ref[0:128, :] = back.astype(BF)
    sb_ref[128:144, :] = extra


def do_state(info, rates, got):
    return pl.pallas_call(
        state_kernel,
        in_specs=[smem(), smem(), vmem()],
        out_specs=[vmem()] * 7,
        out_shape=[
            pltpu.VMEM((BLOCKS, STATE, CH), F32),
            pltpu.VMEM((BLOCKS, STATE, CH), F32),
            pltpu.VMEM((16, CH), F32),
            jax.ShapeDtypeStruct((144, CH), BF),
            jax.ShapeDtypeStruct((144, CH), BF),
            pltpu.VMEM((SUPER, 512), BF),
            pltpu.VMEM((SUPER, 512), F32),
        ],
        compiler_params=params(12),
        cost_estimate=cost(3),
    )(info, rates, *in_vmem(got))


def joined(one_ref, two_ref):
    decay = one_ref[128:129, :].astype(F32) + one_ref[129:130, :].astype(F32)
    return one_ref[0:128, :].astype(F32) + decay * two_ref[0:128, :].astype(F32)


def inner_kernel(info, rates, skips, in_ref, ends_ref, out_ref):
    first = info[3, 0] * HEADS
    tri = lower(BLOCK)
    triu = upper(BLOCK)
    chooser = pick(first, WIDTH)
    column_chooser = pick(first, LANES)
    head_row = lax.broadcasted_iota(jnp.int32, (8, 128), 0)
    head_at = lax.broadcasted_iota(jnp.int32, (8, 128), 1) - first
    row_chooser = ((head_row == head_at) & (head_row < HEADS)).astype(F32).astype(BF)
    skip_row = lane_row([skips[h] for h in range(HEADS)], WIDTH)
    t_at = lax.broadcasted_iota(jnp.int32, (BLOCK, BLOCK), 0)
    s_at = lax.broadcasted_iota(jnp.int32, (BLOCK, BLOCK), 1)
    lane = lax.broadcasted_iota(jnp.int32, (BLOCK, CH), 1)
    owns = [(lane >= h * WIDTH) & (lane < (h + 1) * WIDTH) for h in range(HEADS)]

    def one(j, _):
        rows = pl.ds(pl.multiple_of(j * BLOCK, BLOCK), BLOCK)
        dts = in_ref[rows, 768:896]
        steps = dot(dts, chooser)
        x = in_ref[rows, 0:256].astype(F32)
        gy_low = in_ref[rows, 256:512]
        b = in_ref[rows, 512:640]
        c = in_ref[rows, 640:768]
        columns = dot(tri, dot(dts, column_chooser).astype(BF))
        lines = dot(dot(row_chooser, dts, NT).astype(BF), triu)
        ends = ends_ref[pl.ds(j, 1), :]
        mask = (s_at <= t_at) & (t_at < ends)
        scores = dot(c, b, NT)
        driven = x * steps
        decays = []
        mixes = []
        drives = []
        for h in range(HEADS):
            gap = (columns[:, h * 128 : h * 128 + 128] - lines[h : h + 1, :]) * (-rates[h])
            decay = jnp.exp(jnp.where(mask, gap, NEG))
            decays.append(decay)
            mixes.append((decay * scores).astype(BF))
            drives.append(jnp.where(owns[h], driven, 0.0).astype(BF))
        mix = jnp.concatenate(mixes, axis=1)
        drive = jnp.concatenate(drives, axis=0)
        out_ref[rows, 0:256] = dot(mix, drive) + skip_row * x
        grad_mix = dot(gy_low, drive, NT)
        grad_scores = decays[0] * grad_mix[:, 0:128]
        for h in range(1, HEADS):
            grad_scores = grad_scores + decays[h] * grad_mix[:, h * 128 : h * 128 + 128]
        grad_low = grad_scores.astype(BF)
        back = dot(mix, gy_low, TN)
        grad_drive = jnp.where(owns[0], back[0:128], 0.0)
        for h in range(1, HEADS):
            grad_drive = jnp.where(owns[h], back[h * 128 : h * 128 + 128], grad_drive)
        out_ref[rows, 256:512] = grad_drive * steps + skip_row * gy_low.astype(F32)
        out_ref[rows, 512:640] = dot(grad_low, c, TN)
        out_ref[rows, 640:768] = dot(grad_low, b)
        return 0

    lax.fori_loop(0, BLOCKS, one, 0, unroll=UNROLL)


def do_inner(info, rates, skips, got, ends):
    return pl.pallas_call(
        inner_kernel,
        in_specs=[smem()] * 3 + [vmem()] * 2,
        out_specs=vmem(),
        out_shape=pltpu.VMEM((SUPER, 768), F32),
        compiler_params=params(12),
        cost_estimate=cost(8),
    )(info, rates, skips, *in_vmem(got), ends)


def outer_kernel(
    in_ref, part_ref, low_ref, full_ref, inc_ref, back_ref, factor_ref, f1, f2, b1, b2, out_ref
):
    entering = joined(f1, f2)
    leaving = joined(b1, b2)
    for j in range(BLOCKS):
        rows = slice(j * BLOCK, j * BLOCK + BLOCK)
        b = in_ref[rows, 512:640]
        c = in_ref[rows, 640:768]
        state = (inc_ref[j] + factor_ref[j : j + 1, :] * entering).astype(BF)
        pull = (back_ref[j] + factor_ref[8 + j : 9 + j, :] * leaving).astype(BF)
        y = part_ref[rows, 0:256] + dot(c, state) * full_ref[rows, 256:512]
        gx = part_ref[rows, 256:512] + dot(b, pull) * full_ref[rows, 0:256]
        gb = part_ref[rows, 512:640] + dot(low_ref[rows, 0:256], pull, NT)
        gc = part_ref[rows, 640:768] + dot(low_ref[rows, 256:512], state, NT)
        out_ref[rows, 0:256] = y.astype(BF)
        out_ref[rows, 256:512] = gx.astype(BF)
        out_ref[rows, 512:640] = gb.astype(BF)
        out_ref[rows, 640:768] = gc.astype(BF)


def do_outer(*operands):
    return pl.pallas_call(
        outer_kernel,
        in_specs=[vmem()] * 11,
        out_specs=vmem(),
        out_shape=pltpu.HBM((SUPER, 768), BF),
        compiler_params=params(16),
        cost_estimate=cost(2),
    )(*in_vmem(*operands))


def attention_kernel(
    core, starts, in_ref, own0, own1, own2, oth0, oth1, oth2, start_ref, out_ref, keep_ref, send_ref,
    k_ref, v_ref, kt_ref, vt_ref, near_ref, far_ref, peak_ref, gk_ref, gv_ref, sems
):
    count = SUPER // TQ
    lowest = starts[0] - TK + 1
    places_of = [slice(n * SUPER, n * SUPER + SUPER) for n in range(3)]
    owns = (own2, own1, own0)
    others = (oth2, oth1, oth0)

    def moves(n, first):
        mine, theirs = (owns[n], others[n]) if first else (others[n], owns[n])
        return (
            pltpu.make_async_copy(mine, k_ref.at[places_of[n], :], sems.at[2 * n]),
            pltpu.make_async_copy(theirs, v_ref.at[places_of[n], :], sems.at[2 * n + 1]),
        )

    def on_core(n, first, act):
        @pl.when((lowest < (n + 1) * SUPER) & ((core[0] == 0) == first))
        def _():
            for move in moves(n, first):
                act(move)

    for n in (2, 1, 0):
        on_core(n, True, lambda move: move.start())
        on_core(n, False, lambda move: move.start())
    gk_ref[...] = jnp.zeros_like(gk_ref)
    gv_ref[...] = jnp.zeros_like(gv_ref)
    for n in (2, 1, 0):
        on_core(n, True, lambda move: move.wait())
        on_core(n, False, lambda move: move.wait())

        @pl.when(lowest < (n + 1) * SUPER)
        def _():
            kt_ref[:, places_of[n]] = k_ref[places_of[n], :].T
            vt_ref[:, places_of[n]] = v_ref[places_of[n], :].T

    def tile_sum(p):
        return jnp.sum(p.reshape(p.shape[0] // 8, 8, TQ), axis=0)

    at = lax.broadcasted_iota(jnp.int32, (TQ, TQ), 0)
    here = lax.broadcasted_iota(jnp.int32, (TQ, TQ), 1)
    far_at = lax.broadcasted_iota(jnp.int32, (TK, TQ), 0)
    q_rows = [slice(i * TQ, i * TQ + TQ) for i in range(count)]
    diag = [2 * SUPER + i * TQ for i in range(count)]
    near = [slice(diag[i], diag[i] + TQ) for i in range(count)]
    begins = [start_ref[i : i + 1, :] for i in range(count)]
    gaps = [jnp.maximum(diag[i] - starts[i * TQ], 0) for i in range(count)]
    many = [(gap + HALF - 1) // TK for gap in gaps]
    half = [(gaps[i] > many[i] * TK).astype(jnp.int32) for i in range(count)]

    carries = []
    for i in range(count):
        q = in_ref[q_rows[i], 0:128]
        s = dot(k_ref[near[i], :], q, NT)
        s = jnp.where((at + diag[i] >= begins[i]) & (at <= here), s, NEG)
        peak = jnp.max(s, axis=0, keepdims=True)
        p = jnp.exp((s - peak) * SCALE)
        p_low = p.astype(BF)
        near_ref[i] = p_low
        peak_ref[i, 4:5, :] = peak
        carries.append((peak, tile_sum(p), dot(vt_ref[:, near[i]], p_low)))

    def forward(i, t, carry, size=TK):
        peak, total, att = carry
        base = diag[i] - TK * t - size
        rows = pl.ds(pl.multiple_of(base, HALF), size)
        s = dot(k_ref[rows, :], in_ref[q_rows[i], 0:128], NT)
        s = jnp.where(far_at[0:size] >= begins[i] - base, s, NEG)
        top = jnp.maximum(peak, jnp.max(s, axis=0, keepdims=True))
        alpha = jnp.exp((peak - top) * SCALE)
        p = jnp.exp((s - top) * SCALE)
        p_low = p.astype(BF)
        far_ref[i, t, 0:size, :] = p_low
        peak_ref[i, pl.ds(t, 1), :] = top
        att = att * alpha + dot(vt_ref[:, rows], p_low)
        return top, total * alpha + tile_sum(p), att

    def paired(step, carries):
        shared = many[0]
        for other in many[1:]:
            shared = jnp.minimum(shared, other)
        carries = lax.fori_loop(
            0, shared, lambda t, c: tuple(step(i, t, c[i]) for i in range(count)), tuple(carries)
        )
        results = []
        for i in range(count):
            carry = lax.fori_loop(shared, many[i], lambda t, c: step(i, t, c), carries[i])
            stop = many[i] + half[i]
            results.append(lax.fori_loop(many[i], stop, lambda t, c: step(i, t, c, HALF), carry))
        return results

    carries = paired(forward, carries)

    def grads(i, t, rows, p_low, peak, inverse, delta, ga_turned):
        factor = jnp.exp((peak_ref[i, pl.ds(t, 1), :] - peak) * SCALE) * inverse
        ga = (ga_turned * factor).astype(BF)
        ds = (p_low.astype(F32) * (dot(v_ref[rows, :], ga) - delta * factor)).astype(BF)
        gk_ref[rows, :] += dot(ds, in_ref[q_rows[i], 0:128])
        gv_ref[rows, :] += dot(p_low, ga, NT)
        return dot(kt_ref[:, rows], ds)

    rest = []
    for i in range(count):
        peak, total, att = carries[i]
        ga_turned = in_ref[q_rows[i], 128:256].T.astype(F32)
        inverse = 1.0 / jnp.sum(total, axis=0, keepdims=True)
        att = (att * inverse).astype(BF)
        out_ref[q_rows[i], 0:128] = att.T
        delta = jnp.sum(ga_turned * att.astype(F32), axis=0, keepdims=True)
        state = (peak, inverse, delta, ga_turned)
        rest.append((state, grads(i, 4, near[i], near_ref[i], *state)))

    def backward(i, t, gq, size=TK):
        rows = pl.ds(pl.multiple_of(diag[i] - TK * t - size, HALF), size)
        return gq + grads(i, t, rows, far_ref[i, t, 0:size, :], *rest[i][0])

    for i, gq in enumerate(paired(backward, [gq for _, gq in rest])):
        out_ref[q_rows[i], 128:256] = (gq * SCALE).astype(BF).T

    def store(k_out, v_out):
        k_out[...] = (gk_ref[...] * SCALE).astype(BF)
        v_out[...] = gv_ref[...].astype(BF)

    @pl.when(core[0] == 0)
    def _():
        store(keep_ref, send_ref)

    @pl.when(core[0] != 0)
    def _():
        store(send_ref, keep_ref)


def do_attention(core, starts, *moved):
    span = 3 * SUPER
    count = SUPER // TQ
    return pl.pallas_call(
        attention_kernel,
        in_specs=[smem()] * 2 + [vmem()] + [pl.BlockSpec(memory_space=pl.ANY)] * 6 + [vmem()],
        out_specs=[vmem()] * 3,
        out_shape=[
            pltpu.HBM((SUPER, 256), BF),
            pltpu.HBM((3 * SUPER, 128), BF),
            pltpu.HBM((3 * SUPER, 128), BF),
        ],
        scratch_shapes=[
            pltpu.VMEM((span, 128), BF),
            pltpu.VMEM((span, 128), BF),
            pltpu.VMEM((128, span), BF),
            pltpu.VMEM((128, span), BF),
            pltpu.VMEM((count, TQ, TQ), BF),
            pltpu.VMEM((count, 4, TK, TQ), BF),
            pltpu.VMEM((count, 8, TQ), F32),
            pltpu.VMEM((span, 128), F32),
            pltpu.VMEM((span, 128), F32),
            pltpu.SemaphoreType.DMA((6,)),
        ],
        compiler_params=params(28),
        cost_estimate=cost(ATT),
    )(core, starts, *moved, starts.reshape(SUPER // TQ, TQ))


def shifted(block, distance):
    count = lax.axis_size("z")
    route = [(i, i + distance) for i in range(count) if 0 <= i + distance < count]
    return lax.ppermute(block, "z", route)


def exchange(block):
    return lax.all_to_all(block, GROUP, split_axis=0, concat_axis=0, tiled=True)


def swapped(block):
    return lax.ppermute(block, "core", [(0, 1), (1, 0)])


def per_device(xs, dts, bs, cs, rates, skips, queries, keys, values, lengths, grad_y, grad_attn):
    z, y, core, tp = (lax.axis_index(a) for a in ("z", "y", "core", "tp"))
    inside = (tp // 2) * 4 + core * 2 + tp % 2
    device = y * 8 + inside

    packed_a = do_pack_attention(queries, grad_attn, keys, values)
    packed_a, xs, rates = lax.optimization_barrier((packed_a, xs, rates))
    packed_m = do_pack_mixer(xs, grad_y, bs, cs, dts)
    side = lax.axis_size("tp")
    both = lax.ppermute(
        jnp.stack([rates, skips]),
        ("y", "tp"),
        [(a * side + b, b * side + a) for a in range(side) for b in range(side)],
    )
    mine = lax.dynamic_slice_in_dim(both, inside * HEADS, HEADS, 1)
    my_rates, my_skips = mine[0], mine[1]

    ends = jnp.cumsum(lengths)
    begins = ends - lengths
    base = z * SUPER
    positions = base + jnp.arange(SUPER, dtype=jnp.int32)
    starts = jnp.max(jnp.where(begins[None, :] <= positions[:, None], begins[None, :], 0), axis=1)
    stops = jnp.min(
        jnp.where(ends[None, :] > positions[:, None], ends[None, :], SUPER * 8), axis=1
    )
    block_at = base + jnp.arange(BLOCKS, dtype=jnp.int32) * BLOCK
    last_start = starts[BLOCK - 1 :: BLOCK]
    prior_stop = jnp.min(
        jnp.where(ends[None, :] >= block_at[:, None], ends[None, :], SUPER * 8), axis=1
    )
    entry = jnp.where(block_at > 0, prior_stop - block_at, 0)
    info = jnp.stack(
        [
            last_start - block_at,
            entry,
            (last_start < block_at).astype(jnp.int32),
            jnp.full((BLOCKS,), device, jnp.int32),
        ]
    )
    local_stops = (stops.reshape(BLOCKS, BLOCK) - block_at[:, None]).astype(jnp.int32)

    got_a, packed_m = lax.optimization_barrier((exchange(packed_a), packed_m))
    got_a = got_a.reshape(SUPER, 384)
    own0 = got_a[:, 256:384]
    own1 = shifted(own0, 1)
    own2 = shifted(own1, 1)
    oth0 = swapped(own0)
    packed_m, oth0, my_rates, my_skips = lax.optimization_barrier(
        (packed_m, oth0, my_rates, my_skips)
    )
    got = exchange(packed_m)
    att, keep, send = do_attention(
        jnp.full((1,), core, jnp.int32),
        (starts - (base - 2 * SUPER)).astype(jnp.int32),
        got_a, own0, own1, own2, oth0, swapped(own1), swapped(own2),
    )
    packed_b = do_pack_back(att, keep, swapped(send))
    packed_b, got = lax.optimization_barrier((packed_b, got))
    out_a = exchange(packed_b.reshape(32, ROWS, 640))
    got = got.reshape(SUPER, 896)
    inc, back, factor, send_f, send_b, low, full = do_state(info, my_rates, got)
    got, low = lax.optimization_barrier((got, low))
    f1, f2 = shifted(send_f, 1), shifted(send_f, 2)
    b1, b2 = shifted(send_b, -1), shifted(send_b, -2)
    inner = do_inner(info, my_rates, my_skips, got, local_stops)
    mixed = do_outer(got, inner, low, full, inc, back, factor, f1, f2, b1, b2)
    mixed, out_a = lax.optimization_barrier((mixed, out_a))
    out_m = exchange(mixed.reshape(32, ROWS, 768))
    att, gq, p2, p1, p0 = do_unpack_attention(out_a)
    r1, r2 = shifted(p1, -1), shifted(p2, -2)
    gk, gv = do_add_kv(p0, r1, r2)
    y_out, gx, gb, gc = do_unpack_mixer(out_m)
    return y_out, gx, gb, gc, att, gq, gk, gv


def solution(mesh):
    fine = Mesh(mesh.devices.reshape(-1, 4, 2, 4), ("z", "y", "core", "tp"))
    rows = P(("z", "y", "core", "tp"), None)
    return jax.shard_map(
        per_device,
        mesh=fine,
        in_specs=(rows, rows, rows, rows, P("tp"), P("tp"), rows, rows, rows, P(), rows, rows),
        out_specs=(rows,) * 8,
        check_vma=False,
    )
```
